128 devices in a mesh: mp: 2 (over core), tile: 64 (over y, x, z).
Axes of the slice: x: 4, y: 4, z: 4, core: 2. Of those that a mesh axis runs over, the one named last changes fastest.
Arguments:
- breeze_vectors: float32 [2, 65536], P(None, ('mp', 'tile')), may hold values from -60 to 60
- prior_drag_height: float32 [65536], P(('mp', 'tile')), may hold values from 0.0001 to 0.003
- prior_skin_heat_anomaly: float32 [65536], P(('mp', 'tile')), may hold values from -6 to 6
- sea_flow_vectors: float32 [2, 1024, 256], P(None, ('mp', 'tile')), may hold values from -4 to 4
- skin_heat_anomaly: float32 [1024, 256], P(('mp', 'tile')), may hold values from -6 to 6
- subsurface_heat_anomaly: float32 [1024, 256], P(('mp', 'tile')), may hold values from -4 to -1
- swell_density_table: float32 [36, 32, 1024, 256], P(None, None, ('mp', 'tile')), may hold values from 0.01 to 1
- marine_indicator_grid: int32 [1024, 256], P(('mp', 'tile')), may hold values from 0 to 1, as said below
- home_air_provider: int32 [128, 4608], P(('mp', 'tile')), may hold values from 0 to 511
- home_grid_receiver: int32 [128, 4608], P(('mp', 'tile')), may hold values from 0 to 2047
- flooded_share_factor: float32 [128, 4608], P(('mp', 'tile'))
- border_air_provider: int32 [128, 384], P(('mp', 'tile')), may hold values from 0 to 511
- border_grid_receiver: int32 [128, 384], P(('mp', 'tile')), may hold values from 0 to 2047
- border_share_factor: float32 [128, 384], P(('mp', 'tile'))
- active_couple_tally: int32 [128, 2], P(('mp', 'tile')), may hold values from 0 to 4213, as said below
Outputs:
- currents_out: float32 [2, 1024, 256], P(None, ('mp', 'tile'))
- sst_out: float32 [1024, 256], P(('mp', 'tile'))
- spectrum_out: float32 [36, 32, 1024, 256], P(None, None, ('mp', 'tile'))
- air_drag_height_tenths: float32 [65536], P(('mp', 'tile'))
- air_heat_anomaly_back: float32 [65536], P(('mp', 'tile'))
The draws below stay inside these ranges and needn't reach their ends.
Inputs may be any that keep to these rules, and one draw needn't show every extreme that they name: `marine_indicator_grid`: 1 on every row below 768 and on every row from 896 on; in each column the land, if any, is one run that ends at row 895. Live slots come first in each list. active_couple_tally[0, 0] = 0. active_couple_tally[d, 0] is at most 383 and active_couple_tally[d, 1] at most (383) * 11; both are reached for some d.
All inputs are finite; a program needn't handle non-finite values.
Results may differ from the reference program's by a relative error of at most 0.0001.
Values sent between devices are 32-bit elements; how exact they have to be, the bound alone decides.
A program may use at most 128 MiB of HBM per device.

```python
import math
import jax
import jax.numpy as jnp
import numpy as np
from jax import lax

NDIR = 36
NFREQ = 32
ROWS = 8
GRID_X_EXTENT = 256
WSTEPS = 4
OSTEPS = 4
OWNERS = 128
FINE_DEV = 2048
A_DEV = 512
GRID_Y_EXTENT = 1024
AIR_BOX_TALLY = 65536
SLOTS = 4608
EDGE_SLOTS = 384


def column_pieces(column_index):
    if column_index % 2 == 1:
        return [((column_index - 1) // 2, 1.0)]
    if column_index == 0:
        return [(0, 0.5)]
    return [(column_index // 2 - 1, 0.5), (column_index // 2, 0.5)]


def row_pieces(row_index):
    if row_index % 2 == 1:
        return [((row_index - 1) // 2, 1.0)]
    if row_index == 0:
        return [(0, 0.5)]
    return [(row_index // 2 - 1, 0.5), (row_index // 2, 0.5)]


def own_candidates():
    fine_cells = []
    atmos_cells = []
    fractions = []
    coarse_columns = GRID_X_EXTENT // 2
    for row_index in range(ROWS):
        for column_index in range(GRID_X_EXTENT):
            for coarse_row, row_part in row_pieces(row_index):
                for coarse_column, column_part in column_pieces(column_index):
                    fine_cells.append(row_index * GRID_X_EXTENT + column_index)
                    atmos_cells.append(coarse_row * coarse_columns + coarse_column)
                    fractions.append(row_part * column_part)
    return (np.array(fine_cells, np.int32), np.array(atmos_cells, np.int32), np.array(fractions, np.float32))


def edge_candidates():
    fine_cells = []
    atmos_cells = []
    fractions = []
    coarse_columns = GRID_X_EXTENT // 2
    top_row = ROWS // 2 - 1
    for column_index in range(GRID_X_EXTENT):
        for coarse_column, column_part in column_pieces(column_index):
            fine_cells.append(column_index)
            atmos_cells.append(top_row * coarse_columns + coarse_column)
            fractions.append(0.5 * column_part)
    return (np.array(fine_cells, np.int32), np.array(atmos_cells, np.int32), np.array(fractions, np.float32))


def ocean_grid(key):
    coast_key = jax.random.fold_in(key, 101)
    land_end = GRID_Y_EXTENT * 7 // 8
    coast_row = jax.random.randint(coast_key, (GRID_X_EXTENT,), GRID_Y_EXTENT * 3 // 4, land_end + 1, dtype=jnp.int32)
    row_grid = jnp.arange(GRID_Y_EXTENT, dtype=jnp.int32)[:, None]
    ocean = (row_grid < coast_row[None, :]) | (row_grid >= land_end)
    return ocean.astype(jnp.int32)


def wet_fraction(key, power):
    wet_key = jax.random.fold_in(key, 102)
    uniform_draw = jax.random.uniform(wet_key, (GRID_Y_EXTENT, GRID_X_EXTENT), jnp.float32)
    return (1.0 - 0.5 * uniform_draw ** power).reshape(OWNERS, FINE_DEV)


def live_flags(key, fine_cells, edge_pair):
    ocean = ocean_grid(key).reshape(OWNERS, FINE_DEV)
    flags = ocean[:, jnp.asarray(fine_cells)]
    if edge_pair:
        owner_index = jnp.arange(OWNERS, dtype=jnp.int32)[:, None]
        flags = jnp.where(owner_index > 0, flags, 0)
    return flags.astype(jnp.int32)


def pack_slots(flags, values, filler, capacity):
    position = jnp.cumsum(flags, axis=1) - 1
    target = jnp.where(flags > 0, position, capacity).astype(jnp.int32)
    owner_rows = jnp.broadcast_to(jnp.arange(OWNERS, dtype=jnp.int32)[:, None], flags.shape)
    spread = jnp.broadcast_to(values, flags.shape).astype(filler.dtype)
    return filler.at[owner_rows, target].set(spread, mode='drop')


def draw_marine_indicator_grid(key, part):
    return ocean_grid(key)


def draw_home_air_provider(key, part):
    fill_key = jax.random.fold_in(key, 1)
    fine_cells, atmos_cells, fractions = own_candidates()
    flags = live_flags(key, fine_cells, False)
    filler = jax.random.randint(fill_key, (OWNERS, SLOTS), 0, A_DEV, dtype=jnp.int32)
    return pack_slots(flags, jnp.asarray(atmos_cells)[None, :], filler, SLOTS)


def draw_home_grid_receiver(key, part):
    fill_key = jax.random.fold_in(key, 2)
    fine_cells, atmos_cells, fractions = own_candidates()
    flags = live_flags(key, fine_cells, False)
    filler = jax.random.randint(fill_key, (OWNERS, SLOTS), 0, FINE_DEV, dtype=jnp.int32)
    return pack_slots(flags, jnp.asarray(fine_cells)[None, :], filler, SLOTS)


def draw_flooded_share_factor(key, part):
    fill_key = jax.random.fold_in(key, 3)
    wet = wet_fraction(key, 1.0)
    fine_cells, atmos_cells, fractions = own_candidates()
    flags = live_flags(key, fine_cells, False)
    values = wet[:, jnp.asarray(fine_cells)] * jnp.asarray(fractions)[None, :]
    filler = jax.random.uniform(fill_key, (OWNERS, SLOTS), jnp.float32, 0.1, 1.0)
    return pack_slots(flags, values, filler, SLOTS)


def draw_border_air_provider(key, part):
    fill_key = jax.random.fold_in(key, 4)
    fine_cells, atmos_cells, fractions = edge_candidates()
    flags = live_flags(key, fine_cells, True)
    filler = jax.random.randint(fill_key, (OWNERS, EDGE_SLOTS), 0, A_DEV, dtype=jnp.int32)
    return pack_slots(flags, jnp.asarray(atmos_cells)[None, :], filler, EDGE_SLOTS)


def draw_border_grid_receiver(key, part):
    fill_key = jax.random.fold_in(key, 5)
    fine_cells, atmos_cells, fractions = edge_candidates()
    flags = live_flags(key, fine_cells, True)
    filler = jax.random.randint(fill_key, (OWNERS, EDGE_SLOTS), 0, FINE_DEV, dtype=jnp.int32)
    return pack_slots(flags, jnp.asarray(fine_cells)[None, :], filler, EDGE_SLOTS)


def draw_border_share_factor(key, part):
    fill_key = jax.random.fold_in(key, 6)
    wet = wet_fraction(key, 1.0)
    fine_cells, atmos_cells, fractions = edge_candidates()
    flags = live_flags(key, fine_cells, True)
    values = wet[:, jnp.asarray(fine_cells)] * jnp.asarray(fractions)[None, :]
    filler = jax.random.uniform(fill_key, (OWNERS, EDGE_SLOTS), jnp.float32, 0.1, 1.0)
    return pack_slots(flags, values, filler, EDGE_SLOTS)


def draw_active_couple_tally(key, part):
    own_cells = own_candidates()[0]
    edge_cells = edge_candidates()[0]
    own_total = jnp.sum(live_flags(key, own_cells, False), axis=1)
    edge_total = jnp.sum(live_flags(key, edge_cells, True), axis=1)
    return jnp.stack([edge_total, own_total], axis=1).astype(jnp.int32)


def level_of(stream_key, dims, cuts, low, largest):
    gain = 1.0
    for axis_at, parts in cuts:
        steps = jax.random.uniform(jax.random.fold_in(jax.random.fold_in(stream_key, 6), axis_at), (parts,), jnp.float32, low / len(cuts), largest / len(cuts))
        gain = gain * jnp.repeat(jnp.exp(steps), dims[axis_at] // parts).reshape((-1,) + (1,) * (len(dims) - 1 - axis_at))
    return gain


def centred(key, shape, scale, bound, pieces=(), kind=jnp.bfloat16):
    values = scale * jax.random.normal(key, shape, jnp.float32)
    if pieces:
        values = values * level_of(key, shape, pieces, -0.22, 0.18)
    return jnp.clip(values, -bound, bound).astype(kind)


def setup_inputs(seed: int = 0) -> dict:
    streams_of = jax.random.split(jax.random.key(seed), 16)
    return {
        "breeze_vectors": centred(streams_of[0], (2, AIR_BOX_TALLY), 15.0, 60.0, ((1, 128),), jnp.float32),
        "prior_drag_height": jnp.clip(jnp.exp(math.log(0.003) - 3.4011974 * jax.random.uniform(streams_of[1], (AIR_BOX_TALLY,), jnp.float32) ** level_of(streams_of[1], (AIR_BOX_TALLY,), ((0, 128),), -0.2, 0.2)), 0.0001, 0.003),
        "prior_skin_heat_anomaly": centred(streams_of[2], (AIR_BOX_TALLY,), 1.0, 6.0, ((0, 128),), jnp.float32),
        "sea_flow_vectors": centred(streams_of[3], (2, GRID_Y_EXTENT, GRID_X_EXTENT), 0.5, 4.0, ((1, 128),), jnp.float32),
        "skin_heat_anomaly": centred(streams_of[4], (GRID_Y_EXTENT, GRID_X_EXTENT), 1.0, 6.0, ((0, 128),), jnp.float32),
        "subsurface_heat_anomaly": jnp.clip(-4.0 + 3.0 * jax.random.uniform(streams_of[5], (GRID_Y_EXTENT, GRID_X_EXTENT), jnp.float32) ** level_of(streams_of[5], (GRID_Y_EXTENT, GRID_X_EXTENT), ((0, 128),), -0.2, 0.2), -4.0, -1.0),
        "swell_density_table": jnp.clip(jnp.exp(math.log(1.0) - 4.6051702 * jax.random.uniform(streams_of[6], (NDIR, NFREQ, GRID_Y_EXTENT, GRID_X_EXTENT), jnp.float32) ** level_of(streams_of[6], (NDIR, NFREQ, GRID_Y_EXTENT, GRID_X_EXTENT), ((2, 128),), -0.2, 0.2)), 0.01, 1.0),
        "marine_indicator_grid": draw_marine_indicator_grid(jax.random.fold_in(streams_of[15], 71), 0),
        "home_air_provider": draw_home_air_provider(jax.random.fold_in(streams_of[15], 71), 0),
        "home_grid_receiver": draw_home_grid_receiver(jax.random.fold_in(streams_of[15], 71), 0),
        "flooded_share_factor": draw_flooded_share_factor(jax.random.fold_in(streams_of[15], 71), 0),
        "border_air_provider": draw_border_air_provider(jax.random.fold_in(streams_of[15], 71), 0),
        "border_grid_receiver": draw_border_grid_receiver(jax.random.fold_in(streams_of[15], 71), 0),
        "border_share_factor": draw_border_share_factor(jax.random.fold_in(streams_of[15], 71), 0),
        "active_couple_tally": draw_active_couple_tally(jax.random.fold_in(streams_of[15], 71), 0),
    }


GRAV = 9.81

def spectral_tables(ndir, nfreq):
    angles = (jnp.arange(ndir, dtype=jnp.float32) + 0.5) * (2.0 * math.pi / ndir)
    frequency = 0.04 * jnp.power(jnp.float32(1.1), jnp.arange(nfreq, dtype=jnp.float32))
    cos_table = jnp.cos(angles)[:, None, None, None]
    sin_table = jnp.sin(angles)[:, None, None, None]
    speeds = (GRAV / (2.0 * math.pi * frequency))[None, :, None, None]
    courant = (0.028 / frequency)[None, :, None, None]
    bin_width = (0.1 * frequency * (2.0 * math.pi / ndir))[None, :, None, None]
    return (cos_table, sin_table, speeds, courant, bin_width)

def advect(swell_power_density, haloed_lines, tables):
    cos_table, sin_table, speeds, courant, bin_width = tables
    zero_column = jnp.zeros(swell_power_density.shape[:3] + (1,), swell_power_density.dtype)
    columns = jnp.concatenate([zero_column, swell_power_density, zero_column], axis=3)
    east_pos = courant * jnp.maximum(cos_table, 0.0)
    east_neg = courant * jnp.maximum(-cos_table, 0.0)
    north_pos = courant * jnp.maximum(sin_table, 0.0)
    north_neg = courant * jnp.maximum(-sin_table, 0.0)
    return swell_power_density - east_pos * (swell_power_density - columns[..., :-2]) - east_neg * (swell_power_density - columns[..., 2:]) - north_pos * (swell_power_density - haloed_lines[:, :, :-2]) - north_neg * (swell_power_density - haloed_lines[:, :, 2:])

def wave_source(advected, wind_east, wind_north, marine_indicator, tables):
    cos_table, sin_table, speeds, courant, bin_width = tables
    energy_sum = lax.optimization_barrier(jnp.sum(advected * bin_width, axis=(0, 1)))
    damping = 0.3 * energy_sum / (energy_sum + 1.0)
    wind_along = cos_table * wind_east + sin_table * wind_north
    growth = 0.01 * jnp.maximum(wind_along / speeds - 1.0, 0.0)
    return advected * (1.0 + growth - damping) * marine_indicator

def marine_advance(marine_variable_bundle, haloed_lines, driving_input, drag_damping, subsurface_heat_anomaly, marine_indicator):
    columns = jnp.pad(marine_variable_bundle, ((0, 0), (0, 0), (1, 1)))
    diffusion_operator = haloed_lines[:, 2:] + haloed_lines[:, :-2] + columns[:, :, 2:] + columns[:, :, :-2] - 4.0 * marine_variable_bundle
    east_flow = marine_variable_bundle[0]
    north_flow = marine_variable_bundle[1]
    heat_anomaly = marine_variable_bundle[2]
    new_east = marine_indicator * (east_flow + 0.1 * driving_input[0] + 0.2 * north_flow - 0.05 * east_flow + 0.2 * diffusion_operator[0])
    new_north = marine_indicator * (north_flow + 0.1 * driving_input[1] - 0.2 * east_flow - 0.05 * north_flow + 0.2 * diffusion_operator[1])
    updated_heat_anomaly = marine_indicator * (heat_anomaly + 0.2 * diffusion_operator[2] - 0.05 * drag_damping * (heat_anomaly - subsurface_heat_anomaly))
    return jnp.stack([new_east, new_north, updated_heat_anomaly])

def atmosphere_forcing(breeze_vectors, prior_drag_height):
    drag_factor = (0.4 / jnp.log(10.0 / prior_drag_height)) ** 2
    speed = jnp.sqrt(breeze_vectors[0] * breeze_vectors[0] + breeze_vectors[1] * breeze_vectors[1] + 1.0)
    return jnp.stack([1.2 * drag_factor * speed * breeze_vectors[0], 1.2 * drag_factor * speed * breeze_vectors[1], breeze_vectors[0], breeze_vectors[1]])

def fine_roughness(swell_power_density, drag_damping, tables):
    bin_width = tables[4]
    wave_height = 4.0 * jnp.sqrt(lax.optimization_barrier(jnp.sum(swell_power_density * bin_width, axis=(0, 1))) + 1e-06)
    return 1000.0 * ((0.011 + 0.02 * wave_height) * drag_damping / GRAV + 1.5e-05)

def reference(breeze_vectors, prior_drag_height, prior_skin_heat_anomaly, sea_flow_vectors, skin_heat_anomaly, subsurface_heat_anomaly, swell_density_table, marine_indicator_grid, home_air_provider, home_grid_receiver, flooded_share_factor, border_air_provider, border_grid_receiver, border_share_factor, active_couple_tally):
    forcing_atm = atmosphere_forcing(breeze_vectors, prior_drag_height)
    owner_index = jnp.arange(OWNERS, dtype=jnp.int32)
    own_slot = jnp.arange(SLOTS, dtype=jnp.int32)
    edge_slot = jnp.arange(EDGE_SLOTS, dtype=jnp.int32)
    own_live = jnp.where(own_slot[None, :] < active_couple_tally[:, 1:2], flooded_share_factor, 0.0)
    edge_open = (edge_slot[None, :] < active_couple_tally[:, 0:1]) & (owner_index[:, None] > 0)
    edge_live = jnp.where(edge_open, border_share_factor, 0.0)
    own_source = (owner_index[:, None] * A_DEV + home_air_provider).astype(jnp.int32)
    own_target = (owner_index[:, None] * FINE_DEV + home_grid_receiver).astype(jnp.int32)
    below_owner = jnp.maximum(owner_index - 1, 0)
    edge_source = (below_owner[:, None] * A_DEV + border_air_provider).astype(jnp.int32)
    edge_target = (owner_index[:, None] * FINE_DEV + border_grid_receiver).astype(jnp.int32)
    source_all = jnp.concatenate([own_source, edge_source], axis=1).reshape(-1)
    target_all = jnp.concatenate([own_target, edge_target], axis=1).reshape(-1)
    live_all = jnp.concatenate([own_live, edge_live], axis=1).reshape(-1)
    weighted = forcing_atm[:, source_all] * live_all[None]
    driving_input = jnp.zeros((4, GRID_Y_EXTENT * GRID_X_EXTENT), jnp.float32).at[:, target_all].add(weighted)
    driving_input = driving_input.reshape(4, GRID_Y_EXTENT, GRID_X_EXTENT)
    drag_damping = jnp.sqrt(driving_input[0] * driving_input[0] + driving_input[1] * driving_input[1] + 0.01) / 1.2
    marine_indicator = marine_indicator_grid.astype(jnp.float32)
    marine_variable_bundle = jnp.concatenate([sea_flow_vectors, skin_heat_anomaly[None]], axis=0)
    for _ in range(OSTEPS):
        haloed_lines = jnp.pad(marine_variable_bundle, ((0, 0), (1, 1), (0, 0)))
        marine_variable_bundle = marine_advance(marine_variable_bundle, haloed_lines, driving_input, drag_damping, subsurface_heat_anomaly, marine_indicator)
    tables = spectral_tables(NDIR, NFREQ)
    swell_power_density = swell_density_table
    for _ in range(WSTEPS):
        haloed_lines = jnp.pad(swell_power_density, ((0, 0), (0, 0), (1, 1), (0, 0)))
        swell_power_density = wave_source(advect(swell_power_density, haloed_lines, tables), driving_input[2], driving_input[3], marine_indicator, tables)
    roughness = fine_roughness(swell_power_density, drag_damping, tables)
    fine_fields = jnp.stack([marine_indicator * roughness, marine_indicator * marine_variable_bundle[2], marine_indicator]).reshape(3, -1)
    contribution = fine_fields[:, target_all] * live_all[None]
    accumulated_aggregates = jnp.zeros((3, AIR_BOX_TALLY), jnp.float32).at[:, source_all].add(contribution)
    air_drag_height_tenths = (accumulated_aggregates[0] + 1000.0 * prior_drag_height) / (accumulated_aggregates[2] + 1.0)
    air_heat_anomaly_back = (accumulated_aggregates[1] + prior_skin_heat_anomaly) / (accumulated_aggregates[2] + 1.0)
    return (marine_variable_bundle[:2], marine_variable_bundle[2], swell_power_density, air_drag_height_tenths, air_heat_anomaly_back)
```

```python
import functools
import math

import jax
import jax.numpy as jnp
import numpy as np
from jax import lax
from jax.experimental import pallas as pl
from jax.experimental.pallas import tpu as pltpu
from jax.sharding import PartitionSpec as P

MESH = pl.DeviceIdType.MESH
GRAV = 9.81
NDIR = 36
NFREQ = 32
HALF = NDIR // 2
STEPS = 4
LANES = 128
OWN = 4608
EDGE = 384
LIST = OWN + EDGE
CHUNK = 512
GROUP = 3
GROUPS = HALF // GROUP

F32 = jnp.float32
BF16 = jnp.bfloat16

FREQ = 0.04 * 1.1 ** np.arange(NFREQ)
MU = 0.028 / FREQ
INV_SPEED = 2.0 * math.pi * FREQ / GRAV
WIDTH = 0.1 * FREQ * (2.0 * math.pi / NDIR)
ANGLE = (np.arange(NDIR) + 0.5) * (2.0 * math.pi / NDIR)
COS = np.cos(ANGLE)
SIN = np.sin(ANGLE)


def direction_table():
    return np.stack([COS, SIN, np.abs(COS), np.abs(SIN)], axis=1).reshape(-1).astype(np.float32)


def frequency_table():
    rows = np.stack([MU, INV_SPEED, MU * WIDTH, MU / WIDTH])
    return np.broadcast_to(rows[:, :, None], rows.shape + (LANES,)).astype(np.float32)


def iota(shape, dim):
    return lax.broadcasted_iota(jnp.int32, shape, dim)


def spread(row):
    return jnp.broadcast_to(row, (8, row.shape[-1]))


def split_rows(value):
    coarse = value.astype(BF16).astype(F32)
    return jnp.where(iota(value.shape, 0) < 4, coarse, value - coarse)


def main_kernel(
    axis_sizes,
    dirs_in, tally_in, e_in, breeze, drag, heat, flow, skin, subs, marine,
    own_src, own_tgt, own_w, edge_src, edge_tgt, edge_w, freq_in,
    el, eh, cur_out, sst_out, drag_out, heat_out,
    breeze_v, drag_v, heat_v, flow_v, skin_v, subs_v, marine_v,
    osrc_v, otgt_v, ow_v, esrc_v, etgt_v, ew_v, freq,
    bulk_s, bulk_r, flux_s, flux_r, atm_s, atm_r, sea_s, sea_r, frc_s, frc_r, sum_s, sum_r,
    dirs, tally, hot_src, hot_tgt, live_v, field, ocean, state, gather,
    in_sem, e_sem, bulk_ss, bulk_rs, flux_ss, flux_rs, misc_ss, misc_rs,
):
    mp, tile = lax.axis_index("mp"), lax.axis_index("tile")
    n_mp, n_tile = axis_sizes
    count = n_mp * n_tile
    me = mp * n_tile + tile
    up = lax.rem(me + 1, count)
    down = lax.rem(me + count - 1, count)
    up_id = (lax.div(up, n_tile), lax.rem(up, n_tile))
    down_id = (lax.div(down, n_tile), lax.rem(down, n_tile))
    peers = (up_id, down_id)
    has_below = jnp.where(me > 0, 1.0, 0.0).astype(F32)
    has_above = jnp.where(me < count - 1, 1.0, 0.0).astype(F32)
    flags = (has_below, has_above)
    states = (el, eh)

    barrier = pltpu.get_barrier_semaphore()
    for peer in peers:
        pl.semaphore_signal(barrier, inc=1, device_id=peer, device_id_type=MESH)

    small = [
        (breeze, breeze_v), (drag, drag_v), (heat, heat_v), (flow, flow_v), (skin, skin_v),
        (subs, subs_v), (marine, marine_v), (freq_in, freq), (own_src, osrc_v), (own_tgt, otgt_v),
        (own_w, ow_v), (edge_src, esrc_v), (edge_tgt, etgt_v), (edge_w, ew_v),
        (tally_in, tally),
    ]
    small.insert(0, (dirs_in, dirs))
    loads = [pltpu.make_async_copy(s, v, in_sem.at[i]) for i, (s, v) in enumerate(small)]
    for load in loads[:9]:
        load.start()

    def e_load(c, side, half):
        rows = pl.ds(pl.multiple_of((side * HALF + c * GROUP) * 256, 256), GROUP * 256)
        return pltpu.make_async_copy(
            e_in.at[rows, pl.ds(half * LANES, LANES)], states[half].at[rows], e_sem.at[c, side, half]
        )

    for c in range(GROUPS):
        for side in range(2):
            for half in range(2):
                e_load(c, side, half).start()
    for load in loads[9:]:
        load.start()

    def misc(src, dst, index, peer):
        return pltpu.make_async_remote_copy(
            src, dst, misc_ss.at[index], misc_rs.at[index], device_id=peer, device_id_type=MESH
        )

    for load in loads[:3]:
        load.wait()
    wind = breeze_v[...]
    east, north = wind[0:1, :], wind[1:2, :]
    factor = 0.4 / jnp.log(10.0 / drag_v[...])
    factor = factor * factor
    speed = jnp.sqrt(east * east + north * north + 1.0)
    for h in range(4):
        cut = slice(h * LANES, (h + 1) * LANES)
        push = 1.2 * factor[:, cut] * speed[:, cut]
        atm_s[4 * h : 4 * h + 1, :] = push * east[:, cut]
        atm_s[4 * h + 1 : 4 * h + 2, :] = push * north[:, cut]
        atm_s[4 * h + 2 : 4 * h + 3, :] = east[:, cut]
        atm_s[4 * h + 3 : 4 * h + 4, :] = north[:, cut]

    for load in loads[3:9]:
        load.wait()
    ocean_mask = marine_v[...].astype(F32)
    own_fields = [flow_v[0], flow_v[1], skin_v[...], ocean_mask, subs_v[...]]
    for i, value in enumerate(own_fields):
        sea_s[0, 4 * i : 4 * i + 4, :] = value[4:8, :]
        sea_s[1, 4 * i : 4 * i + 4, :] = value[0:4, :]
        ocean[i, 4:12, :] = value

    pl.semaphore_wait(barrier, 2)

    atm_copy = misc(atm_s, atm_r, 0, up_id)
    atm_copy.start()
    sea_copies = [misc(sea_s.at[i], sea_r.at[i], 1 + i, peers[i]) for i in range(2)]
    for copy in sea_copies:
        copy.start()

    def bulk(t, side, c):
        part = pl.ds(c * GROUP, GROUP)
        return pltpu.make_async_remote_copy(
            bulk_s.at[t, side, part], bulk_r.at[t, side, part], bulk_ss.at[t, side],
            bulk_rs.at[t, side], device_id=peers[side], device_id_type=MESH,
        )

    def bulk_all(t, side):
        return pltpu.make_async_remote_copy(
            bulk_s.at[t, side], bulk_r.at[t, side], bulk_ss.at[t, side],
            bulk_rs.at[t, side], device_id=peers[side], device_id_type=MESH,
        )

    def flux(t, side):
        return pltpu.make_async_remote_copy(
            flux_s.at[t, side], flux_r.at[t, side], flux_ss.at[t, side],
            flux_rs.at[t, side], device_id=peers[side], device_id_type=MESH,
        )

    def pack(t, side, kk, totals, neighbour):
        k = side * HALF + kk
        sine = dirs[4 * k + 3]
        coef = 2 if t == 0 else 0
        if neighbour is not None:
            along = [dirs[4 * k] * neighbour[0][h] + dirs[4 * k + 1] * neighbour[1][h] for h in range(2)]
        out = list(totals)
        for g in range(NFREQ // 8):
            weight = freq[coef, 8 * g : 8 * g + 8, :] * sine
            for h in range(2):
                start = k * 256 + 64 * g + (7 if side == 0 else 0)
                rows = states[h][pl.ds(start, 8, stride=8), :]
                bulk_s[t, side, kk, h, 8 * g : 8 * g + 8, :] = rows
                moved = rows * weight
                out[h] = out[h] + moved
                if neighbour is not None:
                    growth = jnp.maximum(along[h] * freq[1, 8 * g : 8 * g + 8, :] - 0.01, 0.0)
                    out[2 + h] = out[2 + h] + moved * growth
        return tuple(out)

    zero = jnp.zeros((8, LANES), F32)

    def send_flux(t, side, totals):
        for i, total in enumerate(totals):
            flux_s[t, side, i] = total
        if len(totals) == 2:
            flux_s[t, side, 2] = zero
            flux_s[t, side, 3] = zero
        flux(t, side).start()

    def first_group(c, carry):
        out = []
        for side in range(2):
            for half in range(2):
                e_load(c, side, half).wait()
            totals = carry[2 * side : 2 * side + 2]
            totals = lax.fori_loop(
                0, GROUP, lambda i, s, side=side: pack(0, side, c * GROUP + i, s, None), totals
            )
            bulk(0, side, c).start()
            out += list(totals)
        return tuple(out)

    fluxes = lax.fori_loop(0, GROUPS, first_group, (zero,) * 4)
    for side in range(2):
        send_flux(0, side, fluxes[2 * side : 2 * side + 2])

    for load in loads[9:]:
        load.wait()

    def to_fine(offset, size, src, tgt, weight, limit, table):
        at = pl.ds(offset, size)
        slot = iota((1, size), 1)
        live = jnp.where(slot < limit, weight, 0.0)
        live_v[:, at] = live
        low = iota((LANES, size), 0)
        hot_s = jnp.where(low == (src & 127), 1.0, 0.0).astype(BF16)
        hot_t = jnp.where(low == (tgt & 127), 1.0, 0.0).astype(BF16)
        hot_src[:, at] = hot_s
        hot_tgt[:, at] = hot_t
        part = jnp.dot(table, hot_s, preferred_element_type=F32)
        part = part[0:16] + part[16:32]
        part = jnp.where((iota((16, size), 0) >> 2) == (src >> 7), part, 0.0)
        part = part[0:8] + part[8:16]
        part = (part + pltpu.roll(part, 4, 0)) * live
        part = split_rows(part)
        high = tgt >> 7
        left = jnp.concatenate([jnp.where(high == h, part, 0.0) for h in range(16)], axis=0)
        return lax.dot_general(
            left.astype(BF16), hot_t, (((1,), (1,)), ((), ())), preferred_element_type=F32
        )

    def two_parts(value):
        coarse = value.astype(BF16).astype(F32)
        return jnp.concatenate([coarse, value - coarse], axis=0).astype(BF16)

    own_table = two_parts(atm_s[...])

    def own_chunk(c, total):
        offset = pl.multiple_of(c * CHUNK, CHUNK)
        at = pl.ds(offset, CHUNK)
        return total + to_fine(
            offset, CHUNK, osrc_v[:, at], otgt_v[:, at], ow_v[:, at], tally[0, 1] - offset, own_table
        )

    total = lax.fori_loop(0, OWN // CHUNK, own_chunk, jnp.zeros((LANES, LANES), F32))
    atm_copy.wait_recv()
    edge_limit = jnp.where(me > 0, tally[0, 0], 0)
    total = total + to_fine(
        OWN, EDGE, esrc_v[...], etgt_v[...], ew_v[...], edge_limit, two_parts(atm_r[...])
    )
    field[...] = total
    forcing = []
    for i in range(4):
        halves = []
        for h in range(2):
            coarse = field[pl.ds(8 * h + i, 8, stride=16), :]
            halves.append(coarse + field[pl.ds(8 * h + i + 4, 8, stride=16), :])
        forcing.append(halves)
        for h in range(2):
            cut = slice(h * LANES, (h + 1) * LANES)
            frc_s[0, 4 * i : 4 * i + 4, cut] = halves[h][4:8, :]
            frc_s[1, 4 * i : 4 * i + 4, cut] = halves[h][0:4, :]
            if i < 2:
                ocean[5 + i, 4:12, cut] = halves[h]
    frc_copies = [misc(frc_s.at[i], frc_r.at[i], 3 + i, peers[i]) for i in range(2)]
    for copy in frc_copies:
        copy.start()

    cuts = [slice(0, LANES), slice(LANES, 2 * LANES)]
    masks = [ocean_mask[:, cut] for cut in cuts]
    friction = [
        jnp.sqrt(forcing[0][h] * forcing[0][h] + forcing[1][h] * forcing[1][h] + 0.01) / 1.2
        for h in range(2)
    ]
    for h in range(2):
        state[0, h] = 0.01 * masks[h] * forcing[2][h]
        state[1, h] = 0.01 * masks[h] * forcing[3][h]

    row8 = iota((8, LANES), 0)
    lane8 = iota((8, LANES), 1)

    def advect(t):
        sums = (zero,) * 4
        for quadrant in range(4):
            west = quadrant in (0, 3)
            south = quadrant < 2

            def one(kk, sums, west=west, south=south, quadrant=quadrant):
                k = quadrant * 9 + kk
                cosine, sine = dirs[4 * k + 2], dirs[4 * k + 3]
                both = cosine + sine
                if west:
                    cos_l = jnp.where(lane8 > 0, cosine, 0.0)
                    cos_h = jnp.full((8, LANES), cosine, F32)
                else:
                    cos_l = jnp.full((8, LANES), cosine, F32)
                    cos_h = jnp.where(lane8 < LANES - 1, cosine, 0.0)
                sin_v = jnp.where(row8 > 0 if south else row8 < 7, sine, 0.0)
                sums = list(sums)
                for m in range(NFREQ):
                    rows = pl.ds(pl.multiple_of(k * 256 + m * 8, 8), 8)
                    e_l, e_h = el[rows, :], eh[rows, :]
                    turn = 1 if west else LANES - 1
                    r_l, r_h = pltpu.roll(e_l, turn, 1), pltpu.roll(e_h, turn, 1)
                    if west:
                        x_l, x_h = r_l, jnp.where(lane8 == 0, r_l, r_h)
                    else:
                        x_l, x_h = jnp.where(lane8 == LANES - 1, r_h, r_l), r_h
                    shift = 1 if south else 7
                    y_l, y_h = pltpu.roll(e_l, shift, 0), pltpu.roll(e_h, shift, 0)
                    scale = float(WIDTH[m]) if t == 0 else 1.0
                    keep = scale - (scale * float(MU[m])) * both
                    gain = scale * float(MU[m])
                    a_l = keep * e_l + gain * (cos_l * x_l + sin_v * y_l)
                    a_h = keep * e_h + gain * (cos_h * x_h + sin_v * y_h)
                    el[rows, :] = a_l
                    eh[rows, :] = a_h
                    p = 2 * (m % 2)
                    sums[p] = sums[p] + a_l
                    sums[p + 1] = sums[p + 1] + a_h
                return tuple(sums)

            sums = lax.fori_loop(0, 9, one, sums)
        return [sums[0] + sums[2], sums[1] + sums[3]]

    def source(t, sums):
        for side in range(2):
            flux(t, side).wait_recv()
        arrived = []
        for side in range(2):
            arrived.append(
                [spread(jnp.sum(flux_r[t, side, i], axis=0, keepdims=True)) * flags[side] for i in range(4)]
            )
        for h in range(2):
            energy = sums[h] + jnp.where(row8 == 0, arrived[0][h], 0.0)
            energy = energy + jnp.where(row8 == 7, arrived[1][h], 0.0)
            kept = masks[h] * (1.0 - 0.3 * energy / (energy + 1.0))
            state[2, h] = kept
            state[3, h] = kept - 0.01 * masks[h]
        return arrived

    def grow(t, neighbours):
        last = t == STEPS - 1

        def group(c, carry):
            out = []
            for side in range(2):
                def one(i, totals, side=side):
                    kk = c * GROUP + i
                    k = side * HALF + kk
                    cosine, sine = dirs[4 * k], dirs[4 * k + 1]
                    along = [cosine * state[0, h] + sine * state[1, h] for h in range(2)]
                    kept = [state[2, h] for h in range(2)]
                    base = [state[3, h] for h in range(2)]
                    totals = list(totals)
                    for m in range(NFREQ):
                        rows = pl.ds(pl.multiple_of(k * 256 + m * 8, 8), 8)
                        for h in range(2):
                            grown = jnp.maximum(along[h] * float(INV_SPEED[m]) + base[h], kept[h])
                            value = states[h][rows, :] * grown
                            if last:
                                p = 2 * (m % 2) + h
                                totals[p] = totals[p] + value
                                value = value * float(1.0 / WIDTH[m])
                            states[h][rows, :] = value
                    if last:
                        return tuple(totals)
                    return pack(t + 1, side, kk, totals, neighbours[side] if neighbours else None)

                if last:
                    carry = lax.fori_loop(0, GROUP, one, carry)
                else:
                    size = len(carry) // 2
                    totals = lax.fori_loop(0, GROUP, one, carry[size * side : size * side + size])
                    bulk(t + 1, side, c).start()
                    out += list(totals)
            return carry if last else tuple(out)

        return lax.fori_loop(0, GROUPS, group, (zero,) * (8 if neighbours else 4))

    def enter(t):
        last = t == STEPS - 1
        coef = 2 if t == 0 else (3 if last else 0)
        for side in range(2):
            bulk_all(t, side).wait_recv()
            edge = 0 if side == 0 else 7
            rows = [[spread(state[i, h, edge : edge + 1, :]) for h in range(2)] for i in range(4)]

            def one(kk, carry, side=side, edge=edge, rows=rows):
                k = side * HALF + kk
                sine = dirs[4 * k + 3] * flags[side]
                along = [dirs[4 * k] * rows[0][h] + dirs[4 * k + 1] * rows[1][h] for h in range(2)]
                for g in range(NFREQ // 8):
                    part = slice(8 * g, 8 * g + 8)
                    weight = freq[coef, part, :] * sine
                    for h in range(2):
                        grown = jnp.maximum(along[h] * freq[1, part, :] + rows[3][h], rows[2][h])
                        at = pl.ds(k * 256 + 64 * g + edge, 8, stride=8)
                        states[h][at, :] = states[h][at, :] + bulk_r[t, side, kk, h, part, :] * weight * grown
                return carry

            lax.fori_loop(0, HALF, one, 0)

    def run_ocean():
        for copy in sea_copies:
            copy.wait_recv()
        for copy in frc_copies:
            copy.wait_recv()
        for side, first in ((0, 0), (1, 12)):
            for i in range(5):
                ocean[i, first : first + 4, :] = sea_r[side, 4 * i : 4 * i + 4, :] * flags[side]
            for i in range(2):
                ocean[5 + i, first : first + 4, :] = frc_r[side, 4 * i : 4 * i + 4, :] * flags[side]
        u, v, q = ocean[0], ocean[1], ocean[2]
        wet, deep, push_u, push_v = ocean[3], ocean[4], ocean[5], ocean[6]
        rub = 0.05 * (jnp.sqrt(push_u * push_u + push_v * push_v + 0.01) / 1.2)
        lane = iota((16, 2 * LANES), 1)

        def lap(w):
            west = jnp.where(lane == 0, 0.0, pltpu.roll(w, 1, 1))
            east = jnp.where(lane == 2 * LANES - 1, 0.0, pltpu.roll(w, 2 * LANES - 1, 1))
            return pltpu.roll(w, 1, 0) + pltpu.roll(w, 15, 0) + west + east - 4.0 * w

        for _ in range(STEPS):
            u, v, q = (
                wet * (u + 0.1 * push_u + 0.2 * v - 0.05 * u + 0.2 * lap(u)),
                wet * (v + 0.1 * push_v - 0.2 * u - 0.05 * v + 0.2 * lap(v)),
                wet * (q + 0.2 * lap(q) - rub * (q - deep)),
            )
        ocean[0], ocean[1], ocean[2] = u, v, q
        cur_out[0] = ocean[0, 4:12, :]
        cur_out[1] = ocean[1, 4:12, :]
        sst_out[...] = ocean[2, 4:12, :]

    for t in range(STEPS):
        sums = advect(t)
        if t == STEPS - 2:
            run_ocean()
        arrived = source(t, sums)
        neighbours = None
        if t == STEPS - 2:
            neighbours = []
            for side, row in ((0, 0), (1, 3)):
                other = 1 - side
                neighbours.append(
                    [
                        [0.01 * spread(frc_r[other, 4 * i + row : 4 * i + row + 1, cut]) for cut in cuts]
                        for i in (2, 3)
                    ]
                )
        fluxes = grow(t, neighbours)
        if t < STEPS - 1:
            size = len(fluxes) // 2
            for side in range(2):
                send_flux(t + 1, side, fluxes[size * side : size * side + size])
            enter(t)

    for h in range(2):
        energy = fluxes[h] + fluxes[2 + h]
        for side, edge in ((0, 0), (1, 7)):
            extra = state[2, h] * arrived[side][h] + masks[h] * arrived[side][2 + h]
            energy = energy + jnp.where(row8 == edge, extra, 0.0)
        height = 4.0 * jnp.sqrt(energy + 1e-6)
        rough = 1000.0 * ((0.011 + 0.02 * height) * friction[h] / GRAV + 1.5e-5)
        values = [masks[h] * rough, masks[h] * ocean[2, 4:12, cuts[h]], masks[h], zero]
        for i, value in enumerate(values):
            coarse = value.astype(BF16).astype(F32)
            gather[pl.ds(8 * h + i, 8, stride=16), :] = coarse
            gather[pl.ds(8 * h + i + 4, 8, stride=16), :] = value - coarse
    table = gather[...].astype(BF16)

    def to_coarse(at, size, src, tgt):
        part = jnp.dot(table, hot_tgt[:, at], preferred_element_type=F32)
        high = tgt >> 7
        value = jnp.zeros((8, size), F32)
        for h in range(16):
            value = value + jnp.where(high == h, part[8 * h : 8 * h + 8], 0.0)
        value = (value + pltpu.roll(value, 4, 0)) * live_v[:, at]
        value = split_rows(value)
        left = jnp.concatenate([jnp.where((src >> 7) == h, value, 0.0) for h in range(4)], axis=0)
        return lax.dot_general(
            left.astype(BF16), hot_src[:, at], (((1,), (1,)), ((), ())), preferred_element_type=F32
        )

    def joined(value):
        return jnp.concatenate(
            [value[8 * h : 8 * h + 4] + value[8 * h + 4 : 8 * h + 8] for h in range(4)], axis=0
        )

    sum_s[...] = joined(to_coarse(pl.ds(OWN, EDGE), EDGE, esrc_v[...], etgt_v[...]))
    sum_copy = misc(sum_s, sum_r, 5, down_id)
    sum_copy.start()

    def back_chunk(c, total):
        at = pl.ds(pl.multiple_of(c * CHUNK, CHUNK), CHUNK)
        return total + to_coarse(at, CHUNK, osrc_v[:, at], otgt_v[:, at])

    own_sums = joined(lax.fori_loop(0, OWN // CHUNK, back_chunk, jnp.zeros((32, LANES), F32)))

    enter(STEPS - 1)

    sum_copy.wait_recv()
    totals = own_sums + sum_r[...] * has_above
    for h in range(4):
        cut = slice(h * LANES, (h + 1) * LANES)
        share = totals[4 * h + 2 : 4 * h + 3] + 1.0
        drag_out[:, cut] = (totals[4 * h : 4 * h + 1] + 1000.0 * drag_v[:, cut]) / share
        heat_out[:, cut] = (totals[4 * h + 1 : 4 * h + 2] + heat_v[:, cut]) / share

    for copy in [atm_copy, sum_copy] + sea_copies + frc_copies:
        copy.wait_send()
    for t in range(STEPS):
        for side in range(2):
            bulk_all(t, side).wait_send()
            flux(t, side).wait_send()


def write_kernel(el, eh, cur, sst, drag, heat, e_out, cur_out, sst_out, drag_out, heat_out, sems):
    parts = 9
    size = el.shape[0] // parts
    copies = []
    for c in range(parts):
        rows = pl.ds(c * size, size)
        for h, ref in enumerate((el, eh)):
            copies.append((ref.at[rows], e_out.at[rows, pl.ds(h * LANES, LANES)]))
    copies += [(cur, cur_out), (sst, sst_out), (drag, drag_out), (heat, heat_out)]
    copies = [pltpu.make_async_copy(s, d, sems.at[i]) for i, (s, d) in enumerate(copies)]
    for copy in copies:
        copy.start()
    for copy in copies:
        copy.wait()


def per_device(
    axis_sizes, breeze, drag, heat, flow, skin, subs, swell, marine, own_src, own_tgt, own_w,
    edge_src, edge_tgt, edge_w, tally,
):
    ndir, nfreq, rows, columns = swell.shape
    cells = drag.shape[0]
    lines = ndir * nfreq * rows
    swell = swell.reshape(lines, columns)
    hbm_spec = pl.BlockSpec(memory_space=pltpu.HBM)
    vmem_spec = pl.BlockSpec(memory_space=pltpu.VMEM)
    small_out = [((2, rows, columns), F32), ((rows, columns), F32), ((1, cells), F32), ((1, cells), F32)]
    vmem = pltpu.VMEM
    dma = pltpu.SemaphoreType.DMA
    results = pl.pallas_call(
        functools.partial(main_kernel, axis_sizes),
        out_shape=[vmem((lines, LANES), F32)] * 2 + [vmem(s, d) for s, d in small_out],
        in_specs=[hbm_spec] * 17,
        out_specs=[vmem_spec] * 6,
        scratch_shapes=[
            vmem(breeze.shape, F32), vmem((1, cells), F32), vmem((1, cells), F32), vmem(flow.shape, F32),
            vmem(skin.shape, F32), vmem(subs.shape, F32), vmem(marine.shape, jnp.int32),
            vmem((1, OWN), jnp.int32), vmem((1, OWN), jnp.int32), vmem((1, OWN), F32),
            vmem((1, EDGE), jnp.int32), vmem((1, EDGE), jnp.int32), vmem((1, EDGE), F32),
            vmem((4, NFREQ, LANES), F32),
            vmem((STEPS, 2, HALF, 2, NFREQ, LANES), F32),
            vmem((STEPS, 2, HALF, 2, NFREQ, LANES), F32),
            vmem((STEPS, 2, 4, 8, LANES), F32), vmem((STEPS, 2, 4, 8, LANES), F32),
            vmem((16, LANES), F32), vmem((16, LANES), F32),
            vmem((2, 20, columns), F32), vmem((2, 20, columns), F32),
            vmem((2, 16, columns), F32), vmem((2, 16, columns), F32),
            vmem((16, LANES), F32), vmem((16, LANES), F32),
            pltpu.SMEM((4 * NDIR,), F32), pltpu.SMEM((1, 2), jnp.int32),
            vmem((LANES, LIST), BF16), vmem((LANES, LIST), BF16), vmem((1, LIST), F32),
            vmem((LANES, LANES), F32), vmem((7, 16, columns), F32), vmem((4, 2, 8, LANES), F32),
            vmem((LANES, LANES), F32),
            dma((16,)), dma((GROUPS, 2, 2)),
            dma((STEPS, 2)), dma((STEPS, 2)), dma((STEPS, 2)), dma((STEPS, 2)), dma((6,)), dma((6,)),
        ],
        compiler_params=pltpu.CompilerParams(
            collective_id=0, has_side_effects=True, vmem_limit_bytes=36 * 2**20
        ),
        name="coupled_step",
    )(*(pltpu.with_memory_space_constraint(x, pltpu.HBM) for x in (
        jnp.asarray(direction_table()), tally, swell, breeze, drag.reshape(1, cells), heat.reshape(1, cells),
        flow, skin, subs, marine, own_src, own_tgt, own_w, edge_src, edge_tgt, edge_w,
        jnp.asarray(frequency_table()),
    )))
    outs = pl.pallas_call(
        write_kernel,
        out_shape=[jax.ShapeDtypeStruct((lines, columns), F32)]
        + [jax.ShapeDtypeStruct(s, d) for s, d in small_out],
        in_specs=[vmem_spec] * 6,
        out_specs=[hbm_spec] * 5,
        scratch_shapes=[dma((22,))],
        name="write_out",
    )(*results)
    spectrum, currents, sst, drag_out, heat_out = outs
    return (
        currents,
        sst,
        spectrum.reshape(ndir, nfreq, rows, columns),
        drag_out.reshape(cells),
        heat_out.reshape(cells),
    )


def solution(mesh):
    both = ("mp", "tile")
    flat, grid, pair = P(both), P(both, None), P(None, both, None)
    in_specs = (P(None, both), flat, flat, pair, grid, grid, P(None, None, both, None)) + (grid,) * 8
    out_specs = (pair, grid, P(None, None, both, None), flat, flat)
    sizes = (mesh.shape["mp"], mesh.shape["tile"])
    return jax.shard_map(
        functools.partial(per_device, sizes), mesh=mesh, in_specs=in_specs, out_specs=out_specs, check_vma=False
    )
```

```python
import functools
import math

import jax
import jax.numpy as jnp
import numpy as np
from jax import lax
from jax.experimental import pallas as pl
from jax.experimental.pallas import tpu as pltpu
from jax.sharding import PartitionSpec as P

MESH = pl.DeviceIdType.MESH
GRAV = 9.81
NDIR = 36
NFREQ = 32
HALF = NDIR // 2
STEPS = 4
LANES = 128
OWN = 4608
EDGE = 384
LIST = OWN + EDGE
CHUNK = 512
GROUP = 3
GROUPS = HALF // GROUP
EARLY = 3

F32 = jnp.float32
BF16 = jnp.bfloat16

FREQ = 0.04 * 1.1 ** np.arange(NFREQ)
MU = 0.028 / FREQ
INV_SPEED = 2.0 * math.pi * FREQ / GRAV
WIDTH = 0.1 * FREQ * (2.0 * math.pi / NDIR)
ANGLE = (np.arange(NDIR) + 0.5) * (2.0 * math.pi / NDIR)
COS = np.cos(ANGLE)
SIN = np.sin(ANGLE)


def direction_table():
    return np.stack([COS, SIN, np.abs(COS), np.abs(SIN)], axis=1).reshape(-1).astype(np.float32)


def frequency_table():
    rows = np.stack([MU, INV_SPEED, MU * WIDTH, MU / WIDTH])
    return np.broadcast_to(rows[:, :, None], rows.shape + (LANES,)).astype(np.float32)


def iota(shape, dim):
    return lax.broadcasted_iota(jnp.int32, shape, dim)


def spread(row):
    return jnp.broadcast_to(row, (8, row.shape[-1]))


def split_rows(value):
    coarse = value.astype(BF16).astype(F32)
    return jnp.where(iota(value.shape, 0) < 4, coarse, value - coarse)


def main_kernel(
    axis_sizes,
    dirs_in, tally_in, e_in, breeze, drag, heat, flow, skin, subs, marine,
    own_src, own_tgt, own_w, edge_src, edge_tgt, edge_w, freq_in,
    el, eh, cur_out, sst_out, drag_out, heat_out,
    breeze_v, drag_v, heat_v, flow_v, skin_v, subs_v, marine_v,
    osrc_v, otgt_v, ow_v, esrc_v, etgt_v, ew_v, freq,
    bulk_s, bulk_r, flux_s, flux_r, atm_s, atm_r, sea_s, sea_r, frc_s, frc_r, sum_s, sum_r,
    dirs, tally, hot_src, hot_tgt, live_v, field, ocean, state, gather,
    in_sem, e_sem, bulk_ss, bulk_rs, flux_ss, flux_rs, misc_ss, misc_rs,
):
    mp, tile = lax.axis_index("mp"), lax.axis_index("tile")
    n_mp, n_tile = axis_sizes
    count = n_mp * n_tile
    me = mp * n_tile + tile
    up = lax.rem(me + 1, count)
    down = lax.rem(me + count - 1, count)
    up_id = (lax.div(up, n_tile), lax.rem(up, n_tile))
    down_id = (lax.div(down, n_tile), lax.rem(down, n_tile))
    peers = (up_id, down_id)
    sends = (me < count - 1, me > 0)
    receives = (me > 0, me < count - 1)
    states = (el, eh)

    barrier = pltpu.get_barrier_semaphore()
    for side in range(2):
        @pl.when(sends[side])
        def _(side=side):
            pl.semaphore_signal(barrier, inc=1, device_id=peers[side], device_id_type=MESH)

    small = [
        (breeze, breeze_v), (drag, drag_v), (heat, heat_v), (flow, flow_v), (skin, skin_v),
        (subs, subs_v), (marine, marine_v), (freq_in, freq), (own_src, osrc_v), (own_tgt, otgt_v),
        (own_w, ow_v), (edge_src, esrc_v), (edge_tgt, etgt_v), (edge_w, ew_v),
        (tally_in, tally),
    ]
    small.insert(0, (dirs_in, dirs))
    loads = [pltpu.make_async_copy(s, v, in_sem.at[i]) for i, (s, v) in enumerate(small)]
    for load in loads[:9]:
        load.start()

    def e_load(c, side, half):
        rows = pl.ds(pl.multiple_of((side * HALF + c * GROUP) * 256, 256), GROUP * 256)
        return pltpu.make_async_copy(
            e_in.at[rows, pl.ds(half * LANES, LANES)], states[half].at[rows], e_sem.at[c, side, half]
        )

    for c in range(GROUPS):
        for side in range(2):
            for half in range(2):
                e_load(c, side, half).start()
    for load in loads[9:]:
        load.start()

    def misc(src, dst, index, peer):
        return pltpu.make_async_remote_copy(
            src, dst, misc_ss.at[index], misc_rs.at[index], device_id=peer, device_id_type=MESH
        )

    for load in loads[:3]:
        load.wait()
    wind = breeze_v[...]
    east, north = wind[0:1, :], wind[1:2, :]
    factor = 0.4 / jnp.log(10.0 / drag_v[...])
    factor = factor * factor
    speed = jnp.sqrt(east * east + north * north + 1.0)
    for h in range(4):
        cut = slice(h * LANES, (h + 1) * LANES)
        push = 1.2 * factor[:, cut] * speed[:, cut]
        atm_s[4 * h : 4 * h + 1, :] = push * east[:, cut]
        atm_s[4 * h + 1 : 4 * h + 2, :] = push * north[:, cut]
        atm_s[4 * h + 2 : 4 * h + 3, :] = east[:, cut]
        atm_s[4 * h + 3 : 4 * h + 4, :] = north[:, cut]

    for load in loads[3:9]:
        load.wait()
    ocean_mask = marine_v[...].astype(F32)
    own_fields = [flow_v[0], flow_v[1], skin_v[...], ocean_mask, subs_v[...]]
    for i, value in enumerate(own_fields):
        sea_s[0, 4 * i : 4 * i + 4, :] = value[4:8, :]
        sea_s[1, 4 * i : 4 * i + 4, :] = value[0:4, :]
        ocean[i, 4:12, :] = value

    for side in range(2):
        @pl.when(jnp.logical_not(receives[side]))
        def _(side=side):
            sea_r[side] = jnp.zeros(sea_r.shape[1:], F32)
            frc_r[side] = jnp.zeros(frc_r.shape[1:], F32)
            for t in range(STEPS):
                flux_r[t, side] = jnp.zeros(flux_r.shape[2:], F32)
            lone = atm_r if side == 0 else sum_r
            lone[...] = jnp.zeros(lone.shape, F32)

    inner = (me > 0) & (me < count - 1)
    pl.semaphore_wait(barrier, jnp.where(inner, 2, 1).astype(jnp.int32))

    atm_copy = misc(atm_s, atm_r, 0, up_id)
    pl.when(sends[0])(atm_copy.start)
    sea_copies = [misc(sea_s.at[i], sea_r.at[i], 1 + i, peers[i]) for i in range(2)]
    for side in range(2):
        pl.when(sends[side])(sea_copies[side].start)

    def bulk(t, side, c):
        part = pl.ds(c * GROUP, GROUP)
        return pltpu.make_async_remote_copy(
            bulk_s.at[t, side, part], bulk_r.at[t, side, part], bulk_ss.at[t, side],
            bulk_rs.at[t, side], device_id=peers[side], device_id_type=MESH,
        )

    def bulk_all(t, side):
        return pltpu.make_async_remote_copy(
            bulk_s.at[t, side], bulk_r.at[t, side], bulk_ss.at[t, side],
            bulk_rs.at[t, side], device_id=peers[side], device_id_type=MESH,
        )

    def flux(t, side):
        return pltpu.make_async_remote_copy(
            flux_s.at[t, side], flux_r.at[t, side], flux_ss.at[t, side],
            flux_rs.at[t, side], device_id=peers[side], device_id_type=MESH,
        )

    def pack(t, side, kk, totals, neighbour):
        k = side * HALF + kk
        sine = dirs[4 * k + 3]
        coef = 2 if t == 0 else 0
        if neighbour is not None:
            along = [dirs[4 * k] * neighbour[0][h] + dirs[4 * k + 1] * neighbour[1][h] for h in range(2)]
        out = list(totals)
        for g in range(NFREQ // 8):
            weight = freq[coef, 8 * g : 8 * g + 8, :] * sine
            for h in range(2):
                start = k * 256 + 64 * g + (7 if side == 0 else 0)
                rows = states[h][pl.ds(start, 8, stride=8), :]
                bulk_s[t, side, kk, h, 8 * g : 8 * g + 8, :] = rows
                moved = rows * weight
                out[h] = out[h] + moved
                if neighbour is not None:
                    growth = jnp.maximum(along[h] * freq[1, 8 * g : 8 * g + 8, :] - 0.01, 0.0)
                    out[2 + h] = out[2 + h] + moved * growth
        return tuple(out)

    zero = jnp.zeros((8, LANES), F32)

    def send_flux(t, side, totals):
        for i, total in enumerate(totals):
            flux_s[t, side, i] = total
        if len(totals) == 2:
            flux_s[t, side, 2] = zero
            flux_s[t, side, 3] = zero
        pl.when(sends[side])(flux(t, side).start)

    def first_group(c, carry):
        out = []
        for side in range(2):
            for half in range(2):
                e_load(c, side, half).wait()
            totals = carry[2 * side : 2 * side + 2]
            totals = lax.fori_loop(
                0, GROUP, lambda i, s, side=side: pack(0, side, c * GROUP + i, s, None), totals
            )
            pl.when(sends[side] & (c < EARLY))(bulk(0, side, c).start)
            out += list(totals)
        return tuple(out)

    fluxes = lax.fori_loop(0, GROUPS, first_group, (zero,) * 4)
    for side in range(2):
        send_flux(0, side, fluxes[2 * side : 2 * side + 2])
    for c in range(EARLY, GROUPS):
        for side in range(2):
            pl.when(sends[side])(bulk(0, side, c).start)

    for load in loads[9:]:
        load.wait()

    def to_fine(offset, size, src, tgt, weight, limit, table):
        at = pl.ds(offset, size)
        slot = iota((1, size), 1)
        live = jnp.where(slot < limit, weight, 0.0)
        live_v[:, at] = live
        low = iota((LANES, size), 0)
        hot_s = jnp.where(low == (src & 127), 1.0, 0.0).astype(BF16)
        hot_t = jnp.where(low == (tgt & 127), 1.0, 0.0).astype(BF16)
        hot_src[:, at] = hot_s
        hot_tgt[:, at] = hot_t
        part = jnp.dot(table, hot_s, preferred_element_type=F32)
        part = part[0:16] + part[16:32]
        part = jnp.where((iota((16, size), 0) >> 2) == (src >> 7), part, 0.0)
        part = part[0:8] + part[8:16]
        part = (part + pltpu.roll(part, 4, 0)) * live
        part = split_rows(part)
        high = tgt >> 7
        left = jnp.concatenate([jnp.where(high == h, part, 0.0) for h in range(16)], axis=0)
        return lax.dot_general(
            left.astype(BF16), hot_t, (((1,), (1,)), ((), ())), preferred_element_type=F32
        )

    def two_parts(value):
        coarse = value.astype(BF16).astype(F32)
        return jnp.concatenate([coarse, value - coarse], axis=0).astype(BF16)

    own_table = two_parts(atm_s[...])

    def own_chunk(c, total):
        offset = pl.multiple_of(c * CHUNK, CHUNK)
        at = pl.ds(offset, CHUNK)
        return total + to_fine(
            offset, CHUNK, osrc_v[:, at], otgt_v[:, at], ow_v[:, at], tally[0, 1] - offset, own_table
        )

    total = lax.fori_loop(0, OWN // CHUNK, own_chunk, jnp.zeros((LANES, LANES), F32))
    pl.when(receives[0])(atm_copy.wait_recv)
    edge_limit = jnp.where(me > 0, tally[0, 0], 0)
    total = total + to_fine(
        OWN, EDGE, esrc_v[...], etgt_v[...], ew_v[...], edge_limit, two_parts(atm_r[...])
    )
    field[...] = total
    forcing = []
    for i in range(4):
        halves = []
        for h in range(2):
            coarse = field[pl.ds(8 * h + i, 8, stride=16), :]
            halves.append(coarse + field[pl.ds(8 * h + i + 4, 8, stride=16), :])
        forcing.append(halves)
        for h in range(2):
            cut = slice(h * LANES, (h + 1) * LANES)
            frc_s[0, 4 * i : 4 * i + 4, cut] = halves[h][4:8, :]
            frc_s[1, 4 * i : 4 * i + 4, cut] = halves[h][0:4, :]
            if i < 2:
                ocean[5 + i, 4:12, cut] = halves[h]
    frc_copies = [misc(frc_s.at[i], frc_r.at[i], 3 + i, peers[i]) for i in range(2)]
    for side in range(2):
        pl.when(sends[side])(frc_copies[side].start)

    cuts = [slice(0, LANES), slice(LANES, 2 * LANES)]
    masks = [ocean_mask[:, cut] for cut in cuts]
    friction = [
        jnp.sqrt(forcing[0][h] * forcing[0][h] + forcing[1][h] * forcing[1][h] + 0.01) / 1.2
        for h in range(2)
    ]
    for h in range(2):
        state[0, h] = 0.01 * masks[h] * forcing[2][h]
        state[1, h] = 0.01 * masks[h] * forcing[3][h]

    row8 = iota((8, LANES), 0)
    lane8 = iota((8, LANES), 1)

    def advect(t):
        sums = (zero,) * 4
        for quadrant in range(4):
            west = quadrant in (0, 3)
            south = quadrant < 2

            def one(kk, sums, west=west, south=south, quadrant=quadrant):
                k = quadrant * 9 + kk
                cosine, sine = dirs[4 * k + 2], dirs[4 * k + 3]
                both = cosine + sine
                if west:
                    cos_l = jnp.where(lane8 > 0, cosine, 0.0)
                    cos_h = jnp.full((8, LANES), cosine, F32)
                else:
                    cos_l = jnp.full((8, LANES), cosine, F32)
                    cos_h = jnp.where(lane8 < LANES - 1, cosine, 0.0)
                sin_v = jnp.where(row8 > 0 if south else row8 < 7, sine, 0.0)
                sums = list(sums)
                for m in range(NFREQ):
                    rows = pl.ds(pl.multiple_of(k * 256 + m * 8, 8), 8)
                    e_l, e_h = el[rows, :], eh[rows, :]
                    turn = 1 if west else LANES - 1
                    r_l, r_h = pltpu.roll(e_l, turn, 1), pltpu.roll(e_h, turn, 1)
                    if west:
                        x_l, x_h = r_l, jnp.where(lane8 == 0, r_l, r_h)
                    else:
                        x_l, x_h = jnp.where(lane8 == LANES - 1, r_h, r_l), r_h
                    shift = 1 if south else 7
                    y_l, y_h = pltpu.roll(e_l, shift, 0), pltpu.roll(e_h, shift, 0)
                    scale = float(WIDTH[m]) if t == 0 else 1.0
                    keep = scale - (scale * float(MU[m])) * both
                    gain = scale * float(MU[m])
                    a_l = keep * e_l + gain * (cos_l * x_l + sin_v * y_l)
                    a_h = keep * e_h + gain * (cos_h * x_h + sin_v * y_h)
                    el[rows, :] = a_l
                    eh[rows, :] = a_h
                    p = 2 * (m % 2)
                    sums[p] = sums[p] + a_l
                    sums[p + 1] = sums[p + 1] + a_h
                return tuple(sums)

            sums = lax.fori_loop(0, 9, one, sums)
        return [sums[0] + sums[2], sums[1] + sums[3]]

    def source(t, sums):
        for side in range(2):
            pl.when(receives[side])(flux(t, side).wait_recv)
        arrived = []
        for side in range(2):
            arrived.append(
                [spread(jnp.sum(flux_r[t, side, i], axis=0, keepdims=True)) for i in range(4)]
            )
        for h in range(2):
            energy = sums[h] + jnp.where(row8 == 0, arrived[0][h], 0.0)
            energy = energy + jnp.where(row8 == 7, arrived[1][h], 0.0)
            kept = masks[h] * (1.0 - 0.3 * energy / (energy + 1.0))
            state[2, h] = kept
            state[3, h] = kept - 0.01 * masks[h]
        return arrived

    def grow(t, neighbours):
        last = t == STEPS - 1

        def group(c, carry):
            out = []
            for side in range(2):
                def one(i, totals, side=side):
                    kk = c * GROUP + i
                    k = side * HALF + kk
                    cosine, sine = dirs[4 * k], dirs[4 * k + 1]
                    along = [cosine * state[0, h] + sine * state[1, h] for h in range(2)]
                    kept = [state[2, h] for h in range(2)]
                    base = [state[3, h] for h in range(2)]
                    totals = list(totals)
                    for m in range(NFREQ):
                        rows = pl.ds(pl.multiple_of(k * 256 + m * 8, 8), 8)
                        for h in range(2):
                            grown = jnp.maximum(along[h] * float(INV_SPEED[m]) + base[h], kept[h])
                            value = states[h][rows, :] * grown
                            if last:
                                p = 2 * (m % 2) + h
                                totals[p] = totals[p] + value
                                value = value * float(1.0 / WIDTH[m])
                            states[h][rows, :] = value
                    if last:
                        return tuple(totals)
                    return pack(t + 1, side, kk, totals, neighbours[side] if neighbours else None)

                if last:
                    carry = lax.fori_loop(0, GROUP, one, carry)
                else:
                    size = len(carry) // 2
                    totals = lax.fori_loop(0, GROUP, one, carry[size * side : size * side + size])
                    out += list(totals)
            return carry if last else tuple(out)

        return lax.fori_loop(0, GROUPS, group, (zero,) * (8 if neighbours else 4))

    def enter(t):
        last = t == STEPS - 1
        coef = 2 if t == 0 else (3 if last else 0)
        for side in range(2):
            edge = 0 if side == 0 else 7
            def one(kk, carry, side=side, edge=edge):
                k = side * HALF + kk
                sine = dirs[4 * k + 3]
                rows = [[spread(state[i, h, edge : edge + 1, :]) for h in range(2)] for i in range(4)]
                along = [dirs[4 * k] * rows[0][h] + dirs[4 * k + 1] * rows[1][h] for h in range(2)]
                for g in range(NFREQ // 8):
                    part = slice(8 * g, 8 * g + 8)
                    weight = freq[coef, part, :] * sine
                    for h in range(2):
                        grown = jnp.maximum(along[h] * freq[1, part, :] + rows[3][h], rows[2][h])
                        at = pl.ds(k * 256 + 64 * g + edge, 8, stride=8)
                        states[h][at, :] = states[h][at, :] + bulk_r[t, side, kk, h, part, :] * weight * grown
                return carry

            @pl.when(receives[side])
            def _():
                bulk_all(t, side).wait_recv()
                lax.fori_loop(0, HALF, one, 0)

    def run_ocean():
        for side in range(2):
            pl.when(receives[side])(sea_copies[side].wait_recv)
            pl.when(receives[side])(frc_copies[side].wait_recv)
        for side, first in ((0, 0), (1, 12)):
            for i in range(5):
                ocean[i, first : first + 4, :] = sea_r[side, 4 * i : 4 * i + 4, :]
            for i in range(2):
                ocean[5 + i, first : first + 4, :] = frc_r[side, 4 * i : 4 * i + 4, :]
        u, v, q = ocean[0], ocean[1], ocean[2]
        wet, deep, push_u, push_v = ocean[3], ocean[4], ocean[5], ocean[6]
        rub = 0.05 * (jnp.sqrt(push_u * push_u + push_v * push_v + 0.01) / 1.2)
        lane = iota((16, 2 * LANES), 1)

        def lap(w):
            west = jnp.where(lane == 0, 0.0, pltpu.roll(w, 1, 1))
            east = jnp.where(lane == 2 * LANES - 1, 0.0, pltpu.roll(w, 2 * LANES - 1, 1))
            return pltpu.roll(w, 1, 0) + pltpu.roll(w, 15, 0) + west + east - 4.0 * w

        for _ in range(STEPS):
            u, v, q = (
                wet * (u + 0.1 * push_u + 0.2 * v - 0.05 * u + 0.2 * lap(u)),
                wet * (v + 0.1 * push_v - 0.2 * u - 0.05 * v + 0.2 * lap(v)),
                wet * (q + 0.2 * lap(q) - rub * (q - deep)),
            )
        ocean[0], ocean[1], ocean[2] = u, v, q
        cur_out[0] = ocean[0, 4:12, :]
        cur_out[1] = ocean[1, 4:12, :]
        sst_out[...] = ocean[2, 4:12, :]

    for t in range(STEPS):
        sums = advect(t)
        if t == STEPS - 2:
            run_ocean()
        arrived = source(t, sums)
        neighbours = None
        if t == STEPS - 2:
            neighbours = []
            for side, row in ((0, 0), (1, 3)):
                other = 1 - side
                neighbours.append(
                    [
                        [0.01 * spread(frc_r[other, 4 * i + row : 4 * i + row + 1, cut]) for cut in cuts]
                        for i in (2, 3)
                    ]
                )
        fluxes = grow(t, neighbours)
        if t < STEPS - 1:
            size = len(fluxes) // 2
            for side in range(2):
                send_flux(t + 1, side, fluxes[size * side : size * side + size])
            for side in range(2):
                pl.when(sends[side])(bulk_all(t + 1, side).start)
            enter(t)

    for h in range(2):
        energy = fluxes[h] + fluxes[2 + h]
        for side, edge in ((0, 0), (1, 7)):
            extra = state[2, h] * arrived[side][h] + masks[h] * arrived[side][2 + h]
            energy = energy + jnp.where(row8 == edge, extra, 0.0)
        height = 4.0 * jnp.sqrt(energy + 1e-6)
        rough = 1000.0 * ((0.011 + 0.02 * height) * friction[h] / GRAV + 1.5e-5)
        values = [masks[h] * rough, masks[h] * ocean[2, 4:12, cuts[h]], masks[h], zero]
        for i, value in enumerate(values):
            coarse = value.astype(BF16).astype(F32)
            gather[pl.ds(8 * h + i, 8, stride=16), :] = coarse
            gather[pl.ds(8 * h + i + 4, 8, stride=16), :] = value - coarse
    table = gather[...].astype(BF16)

    def to_coarse(at, size, src, tgt):
        part = jnp.dot(table, hot_tgt[:, at], preferred_element_type=F32)
        high = tgt >> 7
        value = jnp.zeros((8, size), F32)
        for h in range(16):
            value = value + jnp.where(high == h, part[8 * h : 8 * h + 8], 0.0)
        value = (value + pltpu.roll(value, 4, 0)) * live_v[:, at]
        value = split_rows(value)
        left = jnp.concatenate([jnp.where((src >> 7) == h, value, 0.0) for h in range(4)], axis=0)
        return lax.dot_general(
            left.astype(BF16), hot_src[:, at], (((1,), (1,)), ((), ())), preferred_element_type=F32
        )

    def joined(value):
        return jnp.concatenate(
            [value[8 * h : 8 * h + 4] + value[8 * h + 4 : 8 * h + 8] for h in range(4)], axis=0
        )

    sum_s[...] = joined(to_coarse(pl.ds(OWN, EDGE), EDGE, esrc_v[...], etgt_v[...]))
    sum_copy = misc(sum_s, sum_r, 5, down_id)
    pl.when(sends[1])(sum_copy.start)

    def back_chunk(c, total):
        at = pl.ds(pl.multiple_of(c * CHUNK, CHUNK), CHUNK)
        return total + to_coarse(at, CHUNK, osrc_v[:, at], otgt_v[:, at])

    own_sums = joined(lax.fori_loop(0, OWN // CHUNK, back_chunk, jnp.zeros((32, LANES), F32)))

    enter(STEPS - 1)

    pl.when(receives[1])(sum_copy.wait_recv)
    totals = own_sums + sum_r[...]
    for h in range(4):
        cut = slice(h * LANES, (h + 1) * LANES)
        share = totals[4 * h + 2 : 4 * h + 3] + 1.0
        drag_out[:, cut] = (totals[4 * h : 4 * h + 1] + 1000.0 * drag_v[:, cut]) / share
        heat_out[:, cut] = (totals[4 * h + 1 : 4 * h + 2] + heat_v[:, cut]) / share

    for side in range(2):
        @pl.when(sends[side])
        def _(side=side):
            for copy in ((atm_copy, sum_copy)[side], sea_copies[side], frc_copies[side]):
                copy.wait_send()
            for t in range(STEPS):
                bulk_all(t, side).wait_send()
                flux(t, side).wait_send()


def write_kernel(el, eh, cur, sst, drag, heat, e_out, cur_out, sst_out, drag_out, heat_out, sems):
    parts = 9
    size = el.shape[0] // parts
    copies = []
    for c in range(parts):
        rows = pl.ds(c * size, size)
        for h, ref in enumerate((el, eh)):
            copies.append((ref.at[rows], e_out.at[rows, pl.ds(h * LANES, LANES)]))
    copies += [(cur, cur_out), (sst, sst_out), (drag, drag_out), (heat, heat_out)]
    copies = [pltpu.make_async_copy(s, d, sems.at[i]) for i, (s, d) in enumerate(copies)]
    for copy in copies:
        copy.start()
    for copy in copies:
        copy.wait()


def per_device(
    axis_sizes, breeze, drag, heat, flow, skin, subs, swell, marine, own_src, own_tgt, own_w,
    edge_src, edge_tgt, edge_w, tally,
):
    ndir, nfreq, rows, columns = swell.shape
    cells = drag.shape[0]
    lines = ndir * nfreq * rows
    swell = swell.reshape(lines, columns)
    hbm_spec = pl.BlockSpec(memory_space=pltpu.HBM)
    vmem_spec = pl.BlockSpec(memory_space=pltpu.VMEM)
    small_out = [((2, rows, columns), F32), ((rows, columns), F32), ((1, cells), F32), ((1, cells), F32)]
    vmem = pltpu.VMEM
    dma = pltpu.SemaphoreType.DMA
    results = pl.pallas_call(
        functools.partial(main_kernel, axis_sizes),
        out_shape=[vmem((lines, LANES), F32)] * 2 + [vmem(s, d) for s, d in small_out],
        in_specs=[hbm_spec] * 17,
        out_specs=[vmem_spec] * 6,
        scratch_shapes=[
            vmem(breeze.shape, F32), vmem((1, cells), F32), vmem((1, cells), F32), vmem(flow.shape, F32),
            vmem(skin.shape, F32), vmem(subs.shape, F32), vmem(marine.shape, jnp.int32),
            vmem((1, OWN), jnp.int32), vmem((1, OWN), jnp.int32), vmem((1, OWN), F32),
            vmem((1, EDGE), jnp.int32), vmem((1, EDGE), jnp.int32), vmem((1, EDGE), F32),
            vmem((4, NFREQ, LANES), F32),
            vmem((STEPS, 2, HALF, 2, NFREQ, LANES), F32),
            vmem((STEPS, 2, HALF, 2, NFREQ, LANES), F32),
            vmem((STEPS, 2, 4, 8, LANES), F32), vmem((STEPS, 2, 4, 8, LANES), F32),
            vmem((16, LANES), F32), vmem((16, LANES), F32),
            vmem((2, 20, columns), F32), vmem((2, 20, columns), F32),
            vmem((2, 16, columns), F32), vmem((2, 16, columns), F32),
            vmem((16, LANES), F32), vmem((16, LANES), F32),
            pltpu.SMEM((4 * NDIR,), F32), pltpu.SMEM((1, 2), jnp.int32),
            vmem((LANES, LIST), BF16), vmem((LANES, LIST), BF16), vmem((1, LIST), F32),
            vmem((LANES, LANES), F32), vmem((7, 16, columns), F32), vmem((4, 2, 8, LANES), F32),
            vmem((LANES, LANES), F32),
            dma((16,)), dma((GROUPS, 2, 2)),
            dma((STEPS, 2)), dma((STEPS, 2)), dma((STEPS, 2)), dma((STEPS, 2)), dma((6,)), dma((6,)),
        ],
        compiler_params=pltpu.CompilerParams(
            collective_id=0, has_side_effects=True, vmem_limit_bytes=36 * 2**20
        ),
        name="coupled_step",
    )(*(pltpu.with_memory_space_constraint(x, pltpu.HBM) for x in (
        jnp.asarray(direction_table()), tally, swell, breeze, drag.reshape(1, cells), heat.reshape(1, cells),
        flow, skin, subs, marine, own_src, own_tgt, own_w, edge_src, edge_tgt, edge_w,
        jnp.asarray(frequency_table()),
    )))
    outs = pl.pallas_call(
        write_kernel,
        out_shape=[jax.ShapeDtypeStruct((lines, columns), F32)]
        + [jax.ShapeDtypeStruct(s, d) for s, d in small_out],
        in_specs=[vmem_spec] * 6,
        out_specs=[hbm_spec] * 5,
        scratch_shapes=[dma((22,))],
        compiler_params=pltpu.CompilerParams(vmem_limit_bytes=4 * 2**20),
        name="write_out",
    )(*(pltpu.with_memory_space_constraint(x, pltpu.VMEM) for x in results))
    spectrum, currents, sst, drag_out, heat_out = outs
    return (
        currents,
        sst,
        spectrum.reshape(ndir, nfreq, rows, columns),
        drag_out.reshape(cells),
        heat_out.reshape(cells),
    )


def solution(mesh):
    both = ("mp", "tile")
    flat, grid, pair = P(both), P(both, None), P(None, both, None)
    in_specs = (P(None, both), flat, flat, pair, grid, grid, P(None, None, both, None)) + (grid,) * 8
    out_specs = (pair, grid, P(None, None, both, None), flat, flat)
    sizes = (mesh.shape["mp"], mesh.shape["tile"])
    return jax.shard_map(
        functools.partial(per_device, sizes), mesh=mesh, in_specs=in_specs, out_specs=out_specs, check_vma=False
    )
```

```python
import functools
import math

import jax
import jax.numpy as jnp
import numpy as np
from jax import lax
from jax.experimental import pallas as pl
from jax.experimental.pallas import tpu as pltpu
from jax.sharding import PartitionSpec as P

MESH = pl.DeviceIdType.MESH
GRAV = 9.81
NDIR = 36
NFREQ = 32
HALF = NDIR // 2
STEPS = 4
LANES = 128
OWN = 4608
EDGE = 384
LIST = OWN + EDGE
CHUNK = 512
AHEAD = 6
PART = 3
EARLY = 9

F32 = jnp.float32
BF16 = jnp.bfloat16

FREQ = 0.04 * 1.1 ** np.arange(NFREQ)
MU = 0.028 / FREQ
INV_SPEED = 2.0 * math.pi * FREQ / GRAV
WIDTH = 0.1 * FREQ * (2.0 * math.pi / NDIR)
ANGLE = (np.arange(NDIR) + 0.5) * (2.0 * math.pi / NDIR)
COS = np.cos(ANGLE)
SIN = np.sin(ANGLE)


def direction_table():
    return np.stack([COS, SIN, np.abs(COS), np.abs(SIN)], axis=1).reshape(-1).astype(np.float32)


def frequency_table():
    rows = np.stack([MU, INV_SPEED, MU * WIDTH, MU / WIDTH])
    return np.broadcast_to(rows[:, :, None], rows.shape + (LANES,)).astype(np.float32)


def iota(shape, dim):
    return lax.broadcasted_iota(jnp.int32, shape, dim)


def spread(row):
    return jnp.broadcast_to(row, (8, row.shape[-1]))


def split_rows(value):
    coarse = value.astype(BF16).astype(F32)
    return jnp.where(iota(value.shape, 0) < 4, coarse, value - coarse)


def main_kernel(
    axis_sizes,
    dirs_in, tally_in, e_in, breeze, drag, heat, flow, skin, subs, marine,
    own_src, own_tgt, own_w, edge_src, edge_tgt, edge_w, freq_in,
    el, eh, cur_out, sst_out, drag_out, heat_out,
    breeze_v, drag_v, heat_v, flow_v, skin_v, subs_v, marine_v,
    osrc_v, otgt_v, ow_v, esrc_v, etgt_v, ew_v, freq,
    bulk_s, bulk_r, flux_s, flux_r, atm_s, atm_r, sea_s, sea_r, frc_s, frc_r, sum_s, sum_r,
    dirs, tally, hot_src, hot_tgt, live_v, field, ocean, state, gather,
    in_sem, e_sem, bulk_ss, bulk_rs, last_ss, last_rs, flux_ss, flux_rs, misc_ss, misc_rs,
):
    mp, tile = lax.axis_index("mp"), lax.axis_index("tile")
    n_mp, n_tile = axis_sizes
    count = n_mp * n_tile
    me = mp * n_tile + tile
    up = lax.rem(me + 1, count)
    down = lax.rem(me + count - 1, count)
    up_id = (lax.div(up, n_tile), lax.rem(up, n_tile))
    down_id = (lax.div(down, n_tile), lax.rem(down, n_tile))
    peers = (up_id, down_id)
    sends = (me < count - 1, me > 0)
    receives = (me > 0, me < count - 1)
    states = (el, eh)

    barrier = pltpu.get_barrier_semaphore()
    for side in range(2):
        @pl.when(sends[side])
        def _(side=side):
            pl.semaphore_signal(barrier, inc=1, device_id=peers[side], device_id_type=MESH)

    small = [
        (breeze, breeze_v), (drag, drag_v), (heat, heat_v), (flow, flow_v), (skin, skin_v),
        (subs, subs_v), (marine, marine_v), (own_src, osrc_v), (own_tgt, otgt_v),
        (own_w, ow_v), (edge_src, esrc_v), (edge_tgt, etgt_v), (edge_w, ew_v),
        (tally_in, tally),
    ]
    small = [(dirs_in, dirs), (freq_in, freq)] + small
    loads = [pltpu.make_async_copy(s, v, in_sem.at[i]) for i, (s, v) in enumerate(small)]
    for load in loads[:9]:
        load.start()

    def e_load(kk, side, half):
        rows = pl.ds(pl.multiple_of((side * HALF + kk) * 256, 256), 256)
        return pltpu.make_async_copy(
            e_in.at[rows, pl.ds(half * LANES, LANES)], states[half].at[rows], e_sem.at[kk, side, half]
        )

    def e_start(kk):
        for side in range(2):
            for half in range(2):
                e_load(kk, side, half).start()

    for kk in range(AHEAD):
        e_start(kk)
    for load in loads[9:]:
        load.start()

    def misc(src, dst, index, peer):
        return pltpu.make_async_remote_copy(
            src, dst, misc_ss.at[index], misc_rs.at[index], device_id=peer, device_id_type=MESH
        )

    for side in range(2):
        @pl.when(jnp.logical_not(receives[side]))
        def _(side=side):
            sea_r[side] = jnp.zeros(sea_r.shape[1:], F32)
            frc_r[side] = jnp.zeros(frc_r.shape[1:], F32)
            for t in range(STEPS):
                flux_r[t, side] = jnp.zeros(flux_r.shape[2:], F32)
            lone = atm_r if side == 0 else sum_r
            lone[...] = jnp.zeros(lone.shape, F32)

    inner = (me > 0) & (me < count - 1)
    pl.semaphore_wait(barrier, jnp.where(inner, 2, 1).astype(jnp.int32))

    def bulk(t, side, kk):
        return pltpu.make_async_remote_copy(
            bulk_s.at[t, side, kk], bulk_r.at[t, side, kk], bulk_ss.at[t, side],
            bulk_rs.at[t, side], device_id=peers[side], device_id_type=MESH,
        )

    def bulk_all(t, side):
        return pltpu.make_async_remote_copy(
            bulk_s.at[t, side], bulk_r.at[t, side], bulk_ss.at[t, side],
            bulk_rs.at[t, side], device_id=peers[side], device_id_type=MESH,
        )

    def last_part(part, side):
        at = pl.ds(part * PART, PART)
        t = STEPS - 1
        return pltpu.make_async_remote_copy(
            bulk_s.at[t, side, at], bulk_r.at[t, side, at], last_ss.at[part, side],
            last_rs.at[part, side], device_id=peers[side], device_id_type=MESH,
        )

    def flux(t, side):
        return pltpu.make_async_remote_copy(
            flux_s.at[t, side], flux_r.at[t, side], flux_ss.at[t, side],
            flux_rs.at[t, side], device_id=peers[side], device_id_type=MESH,
        )

    def pack(t, side, kk, totals, neighbour):
        k = side * HALF + kk
        sine = dirs[4 * k + 3]
        coef = 2 if t == 0 else 0
        if neighbour is not None:
            along = [dirs[4 * k] * neighbour[0][h] + dirs[4 * k + 1] * neighbour[1][h] for h in range(2)]
        out = list(totals)
        for g in range(NFREQ // 8):
            weight = freq[coef, 8 * g : 8 * g + 8, :] * sine
            for h in range(2):
                start = k * 256 + 64 * g + (7 if side == 0 else 0)
                rows = states[h][pl.ds(start, 8, stride=8), :]
                bulk_s[t, side, kk, h, 8 * g : 8 * g + 8, :] = rows
                moved = rows * weight
                out[h] = out[h] + moved
                if neighbour is not None:
                    growth = jnp.maximum(along[h] * freq[1, 8 * g : 8 * g + 8, :] - 0.01, 0.0)
                    out[2 + h] = out[2 + h] + moved * growth
        return tuple(out)

    zero = jnp.zeros((8, LANES), F32)

    def send_flux(t, side, totals):
        rows = [jnp.sum(total, axis=0, keepdims=True) for total in totals]
        rows += [jnp.zeros((1, LANES), F32)] * (4 - len(rows))
        flux_s[t, side] = jnp.concatenate(rows, axis=0)
        pl.when(sends[side])(flux(t, side).start)

    def first(kk, carry, early=False):
        pl.when(kk + AHEAD < HALF)(lambda: e_start(kk + AHEAD))
        out = []
        for side in range(2):
            for half in range(2):
                e_load(kk, side, half).wait()
            out += list(pack(0, side, kk, carry[2 * side : 2 * side + 2], None))
            if early:
                pl.when(sends[side])(bulk(0, side, kk).start)
        return tuple(out)

    for load in loads[:2]:
        load.wait()
    fluxes = lax.fori_loop(0, 4, functools.partial(first, early=True), (zero,) * 4)

    for load in loads[2:4]:
        load.wait()
    wind = breeze_v[...]
    east, north = wind[0:1, :], wind[1:2, :]
    factor = 0.4 / jnp.log(10.0 / drag_v[...])
    factor = factor * factor
    speed = jnp.sqrt(east * east + north * north + 1.0)
    for h in range(4):
        cut = slice(h * LANES, (h + 1) * LANES)
        push = 1.2 * factor[:, cut] * speed[:, cut]
        atm_s[4 * h : 4 * h + 1, :] = push * east[:, cut]
        atm_s[4 * h + 1 : 4 * h + 2, :] = push * north[:, cut]
        atm_s[4 * h + 2 : 4 * h + 3, :] = east[:, cut]
        atm_s[4 * h + 3 : 4 * h + 4, :] = north[:, cut]

    atm_copy = misc(atm_s, atm_r, 0, up_id)
    pl.when(sends[0])(atm_copy.start)

    fluxes = lax.fori_loop(4, EARLY, functools.partial(first, early=True), fluxes)
    fluxes = lax.fori_loop(EARLY, HALF, first, fluxes)
    for side in range(2):
        send_flux(0, side, fluxes[2 * side : 2 * side + 2])

    @pl.loop(EARLY, HALF)
    def _(kk):
        for side in range(2):
            pl.when(sends[side])(bulk(0, side, kk).start)

    for load in loads[4:9]:
        load.wait()
    ocean_mask = marine_v[...].astype(F32)
    own_fields = [flow_v[0], flow_v[1], skin_v[...], ocean_mask, subs_v[...]]
    for i, value in enumerate(own_fields):
        sea_s[0, 4 * i : 4 * i + 4, :] = value[4:8, :]
        sea_s[1, 4 * i : 4 * i + 4, :] = value[0:4, :]
        ocean[i, 4:12, :] = value

    sea_copies = [misc(sea_s.at[i], sea_r.at[i], 1 + i, peers[i]) for i in range(2)]
    for side in range(2):
        pl.when(sends[side])(sea_copies[side].start)

    for load in loads[9:]:
        load.wait()

    def to_fine(offset, size, src, tgt, weight, limit, table):
        at = pl.ds(offset, size)
        slot = iota((1, size), 1)
        live = jnp.where(slot < limit, weight, 0.0)
        live_v[:, at] = live
        low = iota((LANES, size), 0)
        hot_s = jnp.where(low == (src & 127), 1.0, 0.0).astype(BF16)
        hot_t = jnp.where(low == (tgt & 127), 1.0, 0.0).astype(BF16)
        hot_src[:, at] = hot_s
        hot_tgt[:, at] = hot_t
        part = jnp.dot(table, hot_s, preferred_element_type=F32)
        part = part[0:16] + part[16:32]
        part = jnp.where((iota((16, size), 0) >> 2) == (src >> 7), part, 0.0)
        part = part[0:8] + part[8:16]
        part = (part + pltpu.roll(part, 4, 0)) * live
        part = split_rows(part)
        high = tgt >> 7
        left = jnp.concatenate([jnp.where(high == h, part, 0.0) for h in range(16)], axis=0)
        return lax.dot_general(
            left.astype(BF16), hot_t, (((1,), (1,)), ((), ())), preferred_element_type=F32
        )

    def two_parts(value):
        coarse = value.astype(BF16).astype(F32)
        return jnp.concatenate([coarse, value - coarse], axis=0).astype(BF16)

    own_table = two_parts(atm_s[...])

    def own_chunk(c, total):
        offset = pl.multiple_of(c * CHUNK, CHUNK)
        at = pl.ds(offset, CHUNK)
        return total + to_fine(
            offset, CHUNK, osrc_v[:, at], otgt_v[:, at], ow_v[:, at], tally[0, 1] - offset, own_table
        )

    total = lax.fori_loop(0, OWN // CHUNK, own_chunk, jnp.zeros((LANES, LANES), F32))
    pl.when(receives[0])(atm_copy.wait_recv)
    edge_limit = jnp.where(me > 0, tally[0, 0], 0)
    total = total + to_fine(
        OWN, EDGE, esrc_v[...], etgt_v[...], ew_v[...], edge_limit, two_parts(atm_r[...])
    )
    field[...] = total
    forcing = []
    for i in range(4):
        halves = []
        for h in range(2):
            coarse = field[pl.ds(8 * h + i, 8, stride=16), :]
            halves.append(coarse + field[pl.ds(8 * h + i + 4, 8, stride=16), :])
        forcing.append(halves)
        for h in range(2):
            cut = slice(h * LANES, (h + 1) * LANES)
            if i < 2:
                frc_s[0, 3 * i : 3 * i + 3, cut] = halves[h][5:8, :]
                frc_s[1, 3 * i : 3 * i + 3, cut] = halves[h][0:3, :]
                ocean[5 + i, 4:12, cut] = halves[h]
            else:
                frc_s[0, 4 + i : 5 + i, cut] = halves[h][7:8, :]
                frc_s[1, 4 + i : 5 + i, cut] = halves[h][0:1, :]
    frc_copies = [misc(frc_s.at[i], frc_r.at[i], 3 + i, peers[i]) for i in range(2)]
    for side in range(2):
        pl.when(sends[side])(frc_copies[side].start)

    cuts = [slice(0, LANES), slice(LANES, 2 * LANES)]
    masks = [ocean_mask[:, cut] for cut in cuts]
    friction = [
        jnp.sqrt(forcing[0][h] * forcing[0][h] + forcing[1][h] * forcing[1][h] + 0.01) / 1.2
        for h in range(2)
    ]
    for h in range(2):
        state[0, h] = 0.01 * masks[h] * forcing[2][h]
        state[1, h] = 0.01 * masks[h] * forcing[3][h]

    row8 = iota((8, LANES), 0)
    lane8 = iota((8, LANES), 1)

    def advect(t):
        sums = (zero,) * 4
        for quadrant in range(4):
            west = quadrant in (0, 3)
            south = quadrant < 2

            def one(kk, sums, west=west, south=south, quadrant=quadrant):
                k = quadrant * 9 + kk
                cosine, sine = dirs[4 * k + 2], dirs[4 * k + 3]
                both = cosine + sine
                if west:
                    cos_l = jnp.where(lane8 > 0, cosine, 0.0)
                    cos_h = jnp.full((8, LANES), cosine, F32)
                else:
                    cos_l = jnp.full((8, LANES), cosine, F32)
                    cos_h = jnp.where(lane8 < LANES - 1, cosine, 0.0)
                sin_v = jnp.where(row8 > 0 if south else row8 < 7, sine, 0.0)
                sums = list(sums)
                for m in range(NFREQ):
                    rows = pl.ds(pl.multiple_of(k * 256 + m * 8, 8), 8)
                    e_l, e_h = el[rows, :], eh[rows, :]
                    turn = 1 if west else LANES - 1
                    r_l, r_h = pltpu.roll(e_l, turn, 1), pltpu.roll(e_h, turn, 1)
                    if west:
                        x_l, x_h = r_l, jnp.where(lane8 == 0, r_l, r_h)
                    else:
                        x_l, x_h = jnp.where(lane8 == LANES - 1, r_h, r_l), r_h
                    shift = 1 if south else 7
                    y_l, y_h = pltpu.roll(e_l, shift, 0), pltpu.roll(e_h, shift, 0)
                    scale = float(WIDTH[m]) if t == 0 else 1.0
                    keep = scale - (scale * float(MU[m])) * both
                    gain = scale * float(MU[m])
                    a_l = keep * e_l + gain * (cos_l * x_l + sin_v * y_l)
                    a_h = keep * e_h + gain * (cos_h * x_h + sin_v * y_h)
                    el[rows, :] = a_l
                    eh[rows, :] = a_h
                    p = 2 * (m % 2)
                    sums[p] = sums[p] + a_l
                    sums[p + 1] = sums[p + 1] + a_h
                return tuple(sums)

            sums = lax.fori_loop(0, 9, one, sums)
        return [sums[0] + sums[2], sums[1] + sums[3]]

    def source(t, sums):
        for side in range(2):
            pl.when(receives[side])(flux(t, side).wait_recv)
        arrived = []
        for side in range(2):
            arrived.append(
                [spread(flux_r[t, side, i : i + 1, :]) for i in range(4)]
            )
        for h in range(2):
            energy = sums[h] + jnp.where(row8 == 0, arrived[0][h], 0.0)
            energy = energy + jnp.where(row8 == 7, arrived[1][h], 0.0)
            kept = masks[h] * (1.0 - 0.3 * energy / (energy + 1.0))
            state[2, h] = kept
            state[3, h] = kept - 0.01 * masks[h]
        return arrived

    def grow(t, neighbours):
        last = t == STEPS - 1

        def one(kk, carry):
            out = []
            for side in range(2):
                k = side * HALF + kk
                cosine, sine = dirs[4 * k], dirs[4 * k + 1]
                along = [cosine * state[0, h] + sine * state[1, h] for h in range(2)]
                kept = [state[2, h] for h in range(2)]
                base = [state[3, h] for h in range(2)]
                size = len(carry) // 2
                totals = list(carry[size * side : size * side + size])
                for m in range(NFREQ):
                    rows = pl.ds(pl.multiple_of(k * 256 + m * 8, 8), 8)
                    for h in range(2):
                        grown = jnp.maximum(along[h] * float(INV_SPEED[m]) + base[h], kept[h])
                        value = states[h][rows, :] * grown
                        if last:
                            totals[h] = totals[h] + value
                            value = value * float(1.0 / WIDTH[m])
                        states[h][rows, :] = value
                if not last:
                    totals = pack(t + 1, side, kk, totals, neighbours[side] if neighbours else None)
                out += list(totals)
            return tuple(out)

        return lax.fori_loop(0, HALF, one, (zero,) * (8 if neighbours else 4))

    def enter(t):
        last = t == STEPS - 1
        coef = 2 if t == 0 else (3 if last else 0)
        def one(kk, carry, side):
            edge = 0 if side == 0 else 7
            k = side * HALF + kk
            sine = dirs[4 * k + 3]
            rows = [[spread(state[i, h, edge : edge + 1, :]) for h in range(2)] for i in range(4)]
            along = [dirs[4 * k] * rows[0][h] + dirs[4 * k + 1] * rows[1][h] for h in range(2)]
            for g in range(NFREQ // 8):
                part = slice(8 * g, 8 * g + 8)
                weight = freq[coef, part, :] * sine
                for h in range(2):
                    grown = jnp.maximum(along[h] * freq[1, part, :] + rows[3][h], rows[2][h])
                    at = pl.ds(k * 256 + 64 * g + edge, 8, stride=8)
                    states[h][at, :] = states[h][at, :] + bulk_r[t, side, kk, h, part, :] * weight * grown
            return carry

        size = PART if last else HALF

        def arrive(part, carry):
            for side in range(2):
                @pl.when(receives[side])
                def _(side=side):
                    (last_part(part, side) if last else bulk_all(t, side)).wait_recv()
                    lax.fori_loop(part * size, part * size + size, functools.partial(one, side=side), 0)
            return carry

        if last:
            lax.fori_loop(0, HALF // PART, arrive, 0)
        else:
            arrive(0, 0)

    def run_ocean():
        for side in range(2):
            pl.when(receives[side])(sea_copies[side].wait_recv)
            pl.when(receives[side])(frc_copies[side].wait_recv)
        for side, first in ((0, 0), (1, 12)):
            for i in range(5):
                ocean[i, first : first + 4, :] = sea_r[side, 4 * i : 4 * i + 4, :]
            for i in range(2):
                inner_row = first + 1 if side == 0 else first
                ocean[5 + i, inner_row : inner_row + 3, :] = frc_r[side, 3 * i : 3 * i + 3, :]
                outer_row = first if side == 0 else first + 3
                ocean[5 + i, outer_row : outer_row + 1, :] = jnp.zeros((1, 2 * LANES), F32)
        u, v, q = ocean[0], ocean[1], ocean[2]
        wet, deep, push_u, push_v = ocean[3], ocean[4], ocean[5], ocean[6]
        rub = 0.05 * (jnp.sqrt(push_u * push_u + push_v * push_v + 0.01) / 1.2)
        lane = iota((16, 2 * LANES), 1)

        def lap(w):
            west = jnp.where(lane == 0, 0.0, pltpu.roll(w, 1, 1))
            east = jnp.where(lane == 2 * LANES - 1, 0.0, pltpu.roll(w, 2 * LANES - 1, 1))
            return pltpu.roll(w, 1, 0) + pltpu.roll(w, 15, 0) + west + east - 4.0 * w

        for _ in range(STEPS):
            u, v, q = (
                wet * (u + 0.1 * push_u + 0.2 * v - 0.05 * u + 0.2 * lap(u)),
                wet * (v + 0.1 * push_v - 0.2 * u - 0.05 * v + 0.2 * lap(v)),
                wet * (q + 0.2 * lap(q) - rub * (q - deep)),
            )
        ocean[0], ocean[1], ocean[2] = u, v, q
        cur_out[0] = ocean[0, 4:12, :]
        cur_out[1] = ocean[1, 4:12, :]
        sst_out[...] = ocean[2, 4:12, :]

    for t in range(STEPS):
        sums = advect(t)
        if t == STEPS - 2:
            run_ocean()
        arrived = source(t, sums)
        neighbours = None
        if t == STEPS - 2:
            neighbours = []
            for side in range(2):
                other = 1 - side
                neighbours.append(
                    [
                        [0.01 * spread(frc_r[other, 4 + i : 5 + i, cut]) for cut in cuts]
                        for i in (2, 3)
                    ]
                )
        fluxes = grow(t, neighbours)
        if t < STEPS - 1:
            size = len(fluxes) // 2
            for side in range(2):
                send_flux(t + 1, side, fluxes[size * side : size * side + size])
            for side in range(2):
                if t + 1 < STEPS - 1:
                    pl.when(sends[side])(bulk_all(t + 1, side).start)
                else:
                    for part in range(HALF // PART):
                        pl.when(sends[side])(last_part(part, side).start)
            enter(t)

    for h in range(2):
        energy = fluxes[h] + fluxes[2 + h]
        for side, edge in ((0, 0), (1, 7)):
            extra = state[2, h] * arrived[side][h] + masks[h] * arrived[side][2 + h]
            energy = energy + jnp.where(row8 == edge, extra, 0.0)
        height = 4.0 * jnp.sqrt(energy + 1e-6)
        rough = 1000.0 * ((0.011 + 0.02 * height) * friction[h] / GRAV + 1.5e-5)
        values = [masks[h] * rough, masks[h] * ocean[2, 4:12, cuts[h]], masks[h], zero]
        for i, value in enumerate(values):
            coarse = value.astype(BF16).astype(F32)
            gather[pl.ds(8 * h + i, 8, stride=16), :] = coarse
            gather[pl.ds(8 * h + i + 4, 8, stride=16), :] = value - coarse
    table = gather[...].astype(BF16)

    def to_coarse(at, size, src, tgt):
        part = jnp.dot(table, hot_tgt[:, at], preferred_element_type=F32)
        high = tgt >> 7
        value = jnp.zeros((8, size), F32)
        for h in range(16):
            value = value + jnp.where(high == h, part[8 * h : 8 * h + 8], 0.0)
        value = (value + pltpu.roll(value, 4, 0)) * live_v[:, at]
        value = split_rows(value)
        left = jnp.concatenate([jnp.where((src >> 7) == h, value, 0.0) for h in range(4)], axis=0)
        return lax.dot_general(
            left.astype(BF16), hot_src[:, at], (((1,), (1,)), ((), ())), preferred_element_type=F32
        )

    def joined(value):
        return jnp.concatenate(
            [value[8 * h : 8 * h + 4] + value[8 * h + 4 : 8 * h + 8] for h in range(4)], axis=0
        )

    sum_s[...] = joined(to_coarse(pl.ds(OWN, EDGE), EDGE, esrc_v[...], etgt_v[...]))
    sum_copy = misc(sum_s, sum_r, 5, down_id)
    pl.when(sends[1])(sum_copy.start)

    def back_chunk(c, total):
        at = pl.ds(pl.multiple_of(c * CHUNK, CHUNK), CHUNK)
        return total + to_coarse(at, CHUNK, osrc_v[:, at], otgt_v[:, at])

    own_sums = joined(lax.fori_loop(0, OWN // CHUNK, back_chunk, jnp.zeros((32, LANES), F32)))

    enter(STEPS - 1)

    pl.when(receives[1])(sum_copy.wait_recv)
    totals = own_sums + sum_r[...]
    for h in range(4):
        cut = slice(h * LANES, (h + 1) * LANES)
        share = totals[4 * h + 2 : 4 * h + 3] + 1.0
        drag_out[:, cut] = (totals[4 * h : 4 * h + 1] + 1000.0 * drag_v[:, cut]) / share
        heat_out[:, cut] = (totals[4 * h + 1 : 4 * h + 2] + heat_v[:, cut]) / share

    for side in range(2):
        @pl.when(sends[side])
        def _(side=side):
            for copy in ((atm_copy, sum_copy)[side], sea_copies[side], frc_copies[side]):
                copy.wait_send()
            for t in range(STEPS):
                if t < STEPS - 1:
                    bulk_all(t, side).wait_send()
                flux(t, side).wait_send()
            for part in range(HALF // PART):
                last_part(part, side).wait_send()


def write_kernel(el, eh, cur, sst, drag, heat, e_out, cur_out, sst_out, drag_out, heat_out, sems):
    parts = 9
    size = el.shape[0] // parts
    copies = []
    for c in range(parts):
        rows = pl.ds(c * size, size)
        for h, ref in enumerate((el, eh)):
            copies.append((ref.at[rows], e_out.at[rows, pl.ds(h * LANES, LANES)]))
    copies += [(cur, cur_out), (sst, sst_out), (drag, drag_out), (heat, heat_out)]
    copies = [pltpu.make_async_copy(s, d, sems.at[i]) for i, (s, d) in enumerate(copies)]
    for copy in copies:
        copy.start()
    for copy in copies:
        copy.wait()


def per_device(
    axis_sizes, breeze, drag, heat, flow, skin, subs, swell, marine, own_src, own_tgt, own_w,
    edge_src, edge_tgt, edge_w, tally,
):
    ndir, nfreq, rows, columns = swell.shape
    cells = drag.shape[0]
    lines = ndir * nfreq * rows
    swell = swell.reshape(lines, columns)
    hbm_spec = pl.BlockSpec(memory_space=pltpu.HBM)
    vmem_spec = pl.BlockSpec(memory_space=pltpu.VMEM)
    small_out = [((2, rows, columns), F32), ((rows, columns), F32), ((1, cells), F32), ((1, cells), F32)]
    vmem = pltpu.VMEM
    dma = pltpu.SemaphoreType.DMA
    results = pl.pallas_call(
        functools.partial(main_kernel, axis_sizes),
        out_shape=[vmem((lines, LANES), F32)] * 2 + [vmem(s, d) for s, d in small_out],
        in_specs=[hbm_spec] * 17,
        out_specs=[vmem_spec] * 6,
        scratch_shapes=[
            vmem(breeze.shape, F32), vmem((1, cells), F32), vmem((1, cells), F32), vmem(flow.shape, F32),
            vmem(skin.shape, F32), vmem(subs.shape, F32), vmem(marine.shape, jnp.int32),
            vmem((1, OWN), jnp.int32), vmem((1, OWN), jnp.int32), vmem((1, OWN), F32),
            vmem((1, EDGE), jnp.int32), vmem((1, EDGE), jnp.int32), vmem((1, EDGE), F32),
            vmem((4, NFREQ, LANES), F32),
            vmem((STEPS, 2, HALF, 2, NFREQ, LANES), F32),
            vmem((STEPS, 2, HALF, 2, NFREQ, LANES), F32),
            vmem((STEPS, 2, 4, LANES), F32), vmem((STEPS, 2, 4, LANES), F32),
            vmem((16, LANES), F32), vmem((16, LANES), F32),
            vmem((2, 20, columns), F32), vmem((2, 20, columns), F32),
            vmem((2, 8, columns), F32), vmem((2, 8, columns), F32),
            vmem((16, LANES), F32), vmem((16, LANES), F32),
            pltpu.SMEM((4 * NDIR,), F32), pltpu.SMEM((1, 2), jnp.int32),
            vmem((LANES, LIST), BF16), vmem((LANES, LIST), BF16), vmem((1, LIST), F32),
            vmem((LANES, LANES), F32), vmem((7, 16, columns), F32), vmem((4, 2, 8, LANES), F32),
            vmem((LANES, LANES), F32),
            dma((16,)), dma((HALF, 2, 2)),
            dma((STEPS - 1, 2)), dma((STEPS - 1, 2)), dma((HALF // PART, 2)), dma((HALF // PART, 2)),
            dma((STEPS, 2)), dma((STEPS, 2)), dma((6,)), dma((6,)),
        ],
        compiler_params=pltpu.CompilerParams(
            collective_id=0, has_side_effects=True, vmem_limit_bytes=36 * 2**20
        ),
        name="coupled_step",
    )(*(pltpu.with_memory_space_constraint(x, pltpu.HBM) for x in (
        jnp.asarray(direction_table()), tally, swell, breeze, drag.reshape(1, cells), heat.reshape(1, cells),
        flow, skin, subs, marine, own_src, own_tgt, own_w, edge_src, edge_tgt, edge_w,
        jnp.asarray(frequency_table()),
    )))
    outs = pl.pallas_call(
        write_kernel,
        out_shape=[jax.ShapeDtypeStruct((lines, columns), F32)]
        + [jax.ShapeDtypeStruct(s, d) for s, d in small_out],
        in_specs=[vmem_spec] * 6,
        out_specs=[hbm_spec] * 5,
        scratch_shapes=[dma((22,))],
        compiler_params=pltpu.CompilerParams(vmem_limit_bytes=4 * 2**20),
        name="write_out",
    )(*(pltpu.with_memory_space_constraint(x, pltpu.VMEM) for x in results))
    spectrum, currents, sst, drag_out, heat_out = outs
    return (
        currents,
        sst,
        spectrum.reshape(ndir, nfreq, rows, columns),
        drag_out.reshape(cells),
        heat_out.reshape(cells),
    )


def solution(mesh):
    both = ("mp", "tile")
    flat, grid, pair = P(both), P(both, None), P(None, both, None)
    in_specs = (P(None, both), flat, flat, pair, grid, grid, P(None, None, both, None)) + (grid,) * 8
    out_specs = (pair, grid, P(None, None, both, None), flat, flat)
    sizes = (mesh.shape["mp"], mesh.shape["tile"])
    return jax.shard_map(
        functools.partial(per_device, sizes), mesh=mesh, in_specs=in_specs, out_specs=out_specs, check_vma=False
    )
```

```python
import functools
import math

import jax
import jax.numpy as jnp
import numpy as np
from jax import lax
from jax.experimental import pallas as pl
from jax.experimental.pallas import tpu as pltpu
from jax.sharding import PartitionSpec as P

MESH = pl.DeviceIdType.MESH
GRAV = 9.81
NDIR = 36
NFREQ = 32
HALF = NDIR // 2
STEPS = 4
LANES = 128
OWN = 4608
EDGE = 384
LIST = OWN + EDGE
CHUNK = 512
AHEAD = 10
PART = 3
PARTS = HALF // PART
EARLY = 2
SOON = 2

F32 = jnp.float32
BF16 = jnp.bfloat16

FREQ = 0.04 * 1.1 ** np.arange(NFREQ)
MU = 0.028 / FREQ
INV_SPEED = 2.0 * math.pi * FREQ / GRAV
WIDTH = 0.1 * FREQ * (2.0 * math.pi / NDIR)
ANGLE = (np.arange(NDIR) + 0.5) * (2.0 * math.pi / NDIR)
COS = np.cos(ANGLE)
SIN = np.sin(ANGLE)


def direction_table():
    return np.stack([COS, SIN, np.abs(COS), np.abs(SIN)], axis=1).reshape(-1).astype(np.float32)


def frequency_table():
    rows = np.stack([MU, INV_SPEED, MU * WIDTH, MU / WIDTH])
    return np.broadcast_to(rows[:, :, None], rows.shape + (LANES,)).astype(np.float32)


def iota(shape, dim):
    return lax.broadcasted_iota(jnp.int32, shape, dim)


def spread(row):
    return jnp.broadcast_to(row, (8, row.shape[-1]))


def split_rows(value):
    coarse = value.astype(BF16).astype(F32)
    return jnp.where(iota(value.shape, 0) < 4, coarse, value - coarse)


def main_kernel(
    axis_sizes,
    dirs_in, tally_in, e_in, e_rows, breeze, drag, heat, flow, skin, subs, marine,
    own_src, own_tgt, own_w, edge_src, edge_tgt, edge_w, freq_in,
    el, eh, cur_out, sst_out, drag_out, heat_out,
    breeze_v, drag_v, heat_v, flow_v, skin_v, subs_v, marine_v,
    osrc_v, otgt_v, ow_v, esrc_v, etgt_v, ew_v, freq,
    first_r, bulk_s, bulk_r, flux_s, flux_r, atm_s, atm_r, sea_s, sea_r, frc_s, frc_r, sum_s, sum_r,
    dirs, tally, hot_src, hot_tgt, live_v, field, ocean, state, gather,
    in_sem, e_sem, bulk_ss, bulk_rs, flux_ss, flux_rs, misc_ss, misc_rs,
):
    mp, tile = lax.axis_index("mp"), lax.axis_index("tile")
    n_mp, n_tile = axis_sizes
    count = n_mp * n_tile
    me = mp * n_tile + tile
    up = lax.rem(me + 1, count)
    down = lax.rem(me + count - 1, count)
    up_id = (lax.div(up, n_tile), lax.rem(up, n_tile))
    down_id = (lax.div(down, n_tile), lax.rem(down, n_tile))
    peers = (up_id, down_id)
    sends = (me < count - 1, me > 0)
    receives = (me > 0, me < count - 1)
    states = (el, eh)

    barrier = pltpu.get_barrier_semaphore()
    for side in range(2):
        @pl.when(sends[side])
        def _(side=side):
            pl.semaphore_signal(barrier, inc=1, device_id=peers[side], device_id_type=MESH)

    small = [
        (breeze, breeze_v), (drag, drag_v), (heat, heat_v), (flow, flow_v), (skin, skin_v),
        (subs, subs_v), (marine, marine_v), (own_src, osrc_v), (own_tgt, otgt_v),
        (own_w, ow_v), (edge_src, esrc_v), (edge_tgt, etgt_v), (edge_w, ew_v),
        (tally_in, tally),
    ]
    small = [(dirs_in, dirs), (freq_in, freq)] + small
    loads = [pltpu.make_async_copy(s, v, in_sem.at[i]) for i, (s, v) in enumerate(small)]
    for load in loads[:9]:
        load.start()

    def e_load(kk, side, half):
        rows = pl.ds(pl.multiple_of((side * HALF + kk) * 256, 256), 256)
        return pltpu.make_async_copy(
            e_in.at[rows, pl.ds(half * LANES, LANES)], states[half].at[rows], e_sem.at[kk, side, half]
        )

    def e_start(kk):
        for side in range(2):
            for half in range(2):
                e_load(kk, side, half).start()

    for kk in range(AHEAD):
        e_start(kk)
    for load in loads[9:]:
        load.start()

    def misc(src, dst, index, peer):
        return pltpu.make_async_remote_copy(
            src, dst, misc_ss.at[index], misc_rs.at[index], device_id=peer, device_id_type=MESH
        )

    for side in range(2):
        @pl.when(jnp.logical_not(receives[side]))
        def _(side=side):
            sea_r[side] = jnp.zeros(sea_r.shape[1:], F32)
            frc_r[side] = jnp.zeros(frc_r.shape[1:], F32)
            for t in range(STEPS):
                flux_r[t, side] = jnp.zeros(flux_r.shape[2:], F32)
            lone = atm_r if side == 0 else sum_r
            lone[...] = jnp.zeros(lone.shape, F32)

    inner = (me > 0) & (me < count - 1)
    pl.semaphore_wait(barrier, jnp.where(inner, 2, 1).astype(jnp.int32))

    def moving(t, part, side):
        at = pl.ds(part * PART, PART)
        if t == 0:
            src = e_rows.at[pl.ds(side * HALF + part * PART, PART), :, :, 7 if side == 0 else 0]
            dst = first_r.at[side, at]
        else:
            src, dst = bulk_s.at[t - 1, side, at], bulk_r.at[t - 1, side, at]
        return pltpu.make_async_remote_copy(
            src, dst, bulk_ss.at[t, part, side], bulk_rs.at[t, part, side],
            device_id=peers[side], device_id_type=MESH,
        )

    def move(t, start, stop):
        for part in range(start, stop):
            for side in range(2):
                pl.when(sends[side])(moving(t, part, side).start)

    move(0, 0, 1)

    def flux(t, side):
        return pltpu.make_async_remote_copy(
            flux_s.at[t, side], flux_r.at[t, side], flux_ss.at[t, side],
            flux_rs.at[t, side], device_id=peers[side], device_id_type=MESH,
        )

    def pack(t, side, kk, totals, neighbour):
        k = side * HALF + kk
        sine = dirs[4 * k + 3]
        coef = 2 if t == 0 else 0
        if neighbour is not None:
            along = [dirs[4 * k] * neighbour[0][h] + dirs[4 * k + 1] * neighbour[1][h] for h in range(2)]
        out = list(totals)
        for g in range(NFREQ // 8):
            weight = freq[coef, 8 * g : 8 * g + 8, :] * sine
            for h in range(2):
                start = k * 256 + 64 * g + (7 if side == 0 else 0)
                rows = states[h][pl.ds(start, 8, stride=8), :]
                if t > 0:
                    bulk_s[t - 1, side, kk, h, 8 * g : 8 * g + 8, :] = rows
                moved = rows * weight
                out[h] = out[h] + moved
                if neighbour is not None:
                    growth = jnp.maximum(along[h] * freq[1, 8 * g : 8 * g + 8, :] - 0.01, 0.0)
                    out[2 + h] = out[2 + h] + moved * growth
        return tuple(out)

    zero = jnp.zeros((8, LANES), F32)

    def send_flux(t, side, totals):
        rows = [jnp.sum(total, axis=0, keepdims=True) for total in totals]
        rows += [jnp.zeros((1, LANES), F32)] * (4 - len(rows))
        flux_s[t, side] = jnp.concatenate(rows, axis=0)
        pl.when(sends[side])(flux(t, side).start)

    def first(kk, carry):
        pl.when(kk + AHEAD < HALF)(lambda: e_start(kk + AHEAD))
        out = []
        for side in range(2):
            for half in range(2):
                e_load(kk, side, half).wait()
            out += list(pack(0, side, kk, carry[2 * side : 2 * side + 2], None))
        return tuple(out)

    for load in loads[2:4]:
        load.wait()
    wind = breeze_v[...]
    east, north = wind[0:1, :], wind[1:2, :]
    factor = 0.4 / jnp.log(10.0 / drag_v[...])
    factor = factor * factor
    speed = jnp.sqrt(east * east + north * north + 1.0)
    for h in range(4):
        cut = slice(h * LANES, (h + 1) * LANES)
        push = 1.2 * factor[:, cut] * speed[:, cut]
        atm_s[4 * h : 4 * h + 1, :] = push * east[:, cut]
        atm_s[4 * h + 1 : 4 * h + 2, :] = push * north[:, cut]
        atm_s[4 * h + 2 : 4 * h + 3, :] = east[:, cut]
        atm_s[4 * h + 3 : 4 * h + 4, :] = north[:, cut]

    atm_copy = misc(atm_s, atm_r, 0, up_id)
    pl.when(sends[0])(atm_copy.start)
    move(0, 1, EARLY)

    for load in loads[:2]:
        load.wait()
    fluxes = lax.fori_loop(0, HALF, first, (zero,) * 4)
    for side in range(2):
        send_flux(0, side, fluxes[2 * side : 2 * side + 2])

    move(0, EARLY, PARTS)

    for load in loads[4:9]:
        load.wait()
    ocean_mask = marine_v[...].astype(F32)
    own_fields = [flow_v[0], flow_v[1], skin_v[...], ocean_mask, subs_v[...]]
    for i, value in enumerate(own_fields):
        sea_s[0, 4 * i : 4 * i + 4, :] = value[4:8, :]
        sea_s[1, 4 * i : 4 * i + 4, :] = value[0:4, :]
        ocean[i, 4:12, :] = value

    sea_copies = [misc(sea_s.at[i], sea_r.at[i], 1 + i, peers[i]) for i in range(2)]
    for side in range(2):
        pl.when(sends[side])(sea_copies[side].start)

    for load in loads[9:]:
        load.wait()

    def to_fine(offset, size, src, tgt, weight, limit, table):
        at = pl.ds(offset, size)
        slot = iota((1, size), 1)
        live = jnp.where(slot < limit, weight, 0.0)
        live_v[:, at] = live
        low = iota((LANES, size), 0)
        hot_s = jnp.where(low == (src & 127), 1.0, 0.0).astype(BF16)
        hot_t = jnp.where(low == (tgt & 127), 1.0, 0.0).astype(BF16)
        hot_src[:, at] = hot_s
        hot_tgt[:, at] = hot_t
        part = jnp.dot(table, hot_s, preferred_element_type=F32)
        part = part[0:16] + part[16:32]
        part = jnp.where((iota((16, size), 0) >> 2) == (src >> 7), part, 0.0)
        part = part[0:8] + part[8:16]
        part = (part + pltpu.roll(part, 4, 0)) * live
        part = split_rows(part)
        high = tgt >> 7
        left = jnp.concatenate([jnp.where(high == h, part, 0.0) for h in range(16)], axis=0)
        return lax.dot_general(
            left.astype(BF16), hot_t, (((1,), (1,)), ((), ())), preferred_element_type=F32
        )

    def two_parts(value):
        coarse = value.astype(BF16).astype(F32)
        return jnp.concatenate([coarse, value - coarse], axis=0).astype(BF16)

    own_table = two_parts(atm_s[...])

    def own_chunk(c, total):
        offset = pl.multiple_of(c * CHUNK, CHUNK)
        at = pl.ds(offset, CHUNK)
        return total + to_fine(
            offset, CHUNK, osrc_v[:, at], otgt_v[:, at], ow_v[:, at], tally[0, 1] - offset, own_table
        )

    row8 = iota((8, LANES), 0)
    lane8 = iota((8, LANES), 1)

    def enter(t, part):
        last = t == STEPS - 1
        coef = 2 if t == 0 else (3 if last else 0)
        def one(kk, carry, side):
            edge = 0 if side == 0 else 7
            k = side * HALF + kk
            sine = dirs[4 * k + 3]
            rows = [[spread(state[i, h, edge : edge + 1, :]) for h in range(2)] for i in range(4)]
            along = [dirs[4 * k] * rows[0][h] + dirs[4 * k + 1] * rows[1][h] for h in range(2)]
            for g in range(NFREQ // 8):
                cut = slice(8 * g, 8 * g + 8)
                weight = freq[coef, cut, :] * sine
                for h in range(2):
                    grown = jnp.maximum(along[h] * freq[1, cut, :] + rows[3][h], rows[2][h])
                    at = pl.ds(k * 256 + 64 * g + edge, 8, stride=8)
                    if t == 0:
                        came = first_r[side, kk, cut, h, 0, :]
                    else:
                        came = bulk_r[t - 1, side, kk, h, cut, :]
                    states[h][at, :] = states[h][at, :] + came * weight * grown
            return carry

        for side in range(2):
            @pl.when(receives[side])
            def _(side=side):
                moving(t, part, side).wait_recv()
                lax.fori_loop(part * PART, part * PART + PART, functools.partial(one, side=side), 0)

    def advect(t):
        sums = (zero,) * 4
        for pair in range(2):
            def one(kk, sums, side, pair=pair):
                west = side == pair
                south = side == 0
                k = side * HALF + kk
                cosine, sine = dirs[4 * k + 2], dirs[4 * k + 3]
                both = cosine + sine
                if west:
                    cos_l = jnp.where(lane8 > 0, cosine, 0.0)
                    cos_h = jnp.full((8, LANES), cosine, F32)
                else:
                    cos_l = jnp.full((8, LANES), cosine, F32)
                    cos_h = jnp.where(lane8 < LANES - 1, cosine, 0.0)
                sin_v = jnp.where(row8 > 0 if south else row8 < 7, sine, 0.0)
                sums = list(sums)
                for m in range(NFREQ):
                    rows = pl.ds(pl.multiple_of(k * 256 + m * 8, 8), 8)
                    e_l, e_h = el[rows, :], eh[rows, :]
                    turn = 1 if west else LANES - 1
                    r_l, r_h = pltpu.roll(e_l, turn, 1), pltpu.roll(e_h, turn, 1)
                    if west:
                        x_l, x_h = r_l, jnp.where(lane8 == 0, r_l, r_h)
                    else:
                        x_l, x_h = jnp.where(lane8 == LANES - 1, r_h, r_l), r_h
                    shift = 1 if south else 7
                    y_l, y_h = pltpu.roll(e_l, shift, 0), pltpu.roll(e_h, shift, 0)
                    scale = float(WIDTH[m]) if t == 0 else 1.0
                    keep = scale - (scale * float(MU[m])) * both
                    gain = scale * float(MU[m])
                    a_l = keep * e_l + gain * (cos_l * x_l + sin_v * y_l)
                    a_h = keep * e_h + gain * (cos_h * x_h + sin_v * y_h)
                    el[rows, :] = a_l
                    eh[rows, :] = a_h
                    p = 2 * (m % 2)
                    sums[p] = sums[p] + a_l
                    sums[p + 1] = sums[p + 1] + a_h
                return tuple(sums)

            def part(p, sums, pair=pair, one=one):
                p = p + pair * (PARTS // 2)
                if t > 0:
                    enter(t - 1, p)
                for side in range(2):
                    sums = lax.fori_loop(p * PART, p * PART + PART, functools.partial(one, side=side), sums)
                return sums

            sums = lax.fori_loop(0, PARTS // 2, part, sums)
        return [sums[0] + sums[2], sums[1] + sums[3]]

    def source(t, sums):
        for side in range(2):
            pl.when(receives[side])(flux(t, side).wait_recv)
        arrived = []
        for side in range(2):
            arrived.append(
                [spread(flux_r[t, side, i : i + 1, :]) for i in range(4)]
            )
        for h in range(2):
            energy = sums[h] + jnp.where(row8 == 0, arrived[0][h], 0.0)
            energy = energy + jnp.where(row8 == 7, arrived[1][h], 0.0)
            kept = masks[h] * (1.0 - 0.3 * energy / (energy + 1.0))
            state[2, h] = kept
            state[3, h] = kept - 0.01 * masks[h]
        return arrived

    def grow(t, neighbours):
        last = t == STEPS - 1

        def one(kk, carry):
            out = []
            for side in range(2):
                k = side * HALF + kk
                cosine, sine = dirs[4 * k], dirs[4 * k + 1]
                along = [cosine * state[0, h] + sine * state[1, h] for h in range(2)]
                kept = [state[2, h] for h in range(2)]
                base = [state[3, h] for h in range(2)]
                size = len(carry) // 2
                totals = list(carry[size * side : size * side + size])
                for m in range(NFREQ):
                    rows = pl.ds(pl.multiple_of(k * 256 + m * 8, 8), 8)
                    for h in range(2):
                        grown = jnp.maximum(along[h] * float(INV_SPEED[m]) + base[h], kept[h])
                        value = states[h][rows, :] * grown
                        if last:
                            totals[h] = totals[h] + value
                            value = value * float(1.0 / WIDTH[m])
                        states[h][rows, :] = value
                if not last:
                    totals = pack(t + 1, side, kk, totals, neighbours[side] if neighbours else None)
                out += list(totals)
            return tuple(out)

        totals = (zero,) * (8 if neighbours else 4)
        if last:
            return lax.fori_loop(0, HALF, one, totals)
        totals = lax.fori_loop(0, SOON * PART, one, totals)
        move(t + 1, 0, SOON)
        return lax.fori_loop(SOON * PART, HALF, one, totals)

    def run_ocean():
        for side in range(2):
            pl.when(receives[side])(sea_copies[side].wait_recv)
            pl.when(receives[side])(frc_copies[side].wait_recv)
        for side, first in ((0, 0), (1, 12)):
            for i in range(5):
                ocean[i, first : first + 4, :] = sea_r[side, 4 * i : 4 * i + 4, :]
            for i in range(2):
                inner_row = first + 1 if side == 0 else first
                ocean[5 + i, inner_row : inner_row + 3, :] = frc_r[side, 3 * i : 3 * i + 3, :]
                outer_row = first if side == 0 else first + 3
                ocean[5 + i, outer_row : outer_row + 1, :] = jnp.zeros((1, 2 * LANES), F32)
        u, v, q = ocean[0], ocean[1], ocean[2]
        wet, deep, push_u, push_v = ocean[3], ocean[4], ocean[5], ocean[6]
        rub = 0.05 * (jnp.sqrt(push_u * push_u + push_v * push_v + 0.01) / 1.2)
        lane = iota((16, 2 * LANES), 1)

        def lap(w):
            west = jnp.where(lane == 0, 0.0, pltpu.roll(w, 1, 1))
            east = jnp.where(lane == 2 * LANES - 1, 0.0, pltpu.roll(w, 2 * LANES - 1, 1))
            return pltpu.roll(w, 1, 0) + pltpu.roll(w, 15, 0) + west + east - 4.0 * w

        for _ in range(STEPS):
            u, v, q = (
                wet * (u + 0.1 * push_u + 0.2 * v - 0.05 * u + 0.2 * lap(u)),
                wet * (v + 0.1 * push_v - 0.2 * u - 0.05 * v + 0.2 * lap(v)),
                wet * (q + 0.2 * lap(q) - rub * (q - deep)),
            )
        ocean[0], ocean[1], ocean[2] = u, v, q
        cur_out[0] = ocean[0, 4:12, :]
        cur_out[1] = ocean[1, 4:12, :]
        sst_out[...] = ocean[2, 4:12, :]

    total = lax.fori_loop(0, OWN // CHUNK, own_chunk, jnp.zeros((LANES, LANES), F32))
    sums = advect(0)
    pl.when(receives[0])(atm_copy.wait_recv)
    edge_limit = jnp.where(me > 0, tally[0, 0], 0)
    total = total + to_fine(
        OWN, EDGE, esrc_v[...], etgt_v[...], ew_v[...], edge_limit, two_parts(atm_r[...])
    )
    field[...] = total
    forcing = []
    for i in range(4):
        halves = []
        for h in range(2):
            coarse = field[pl.ds(8 * h + i, 8, stride=16), :]
            halves.append(coarse + field[pl.ds(8 * h + i + 4, 8, stride=16), :])
        forcing.append(halves)
        for h in range(2):
            cut = slice(h * LANES, (h + 1) * LANES)
            if i < 2:
                frc_s[0, 3 * i : 3 * i + 3, cut] = halves[h][5:8, :]
                frc_s[1, 3 * i : 3 * i + 3, cut] = halves[h][0:3, :]
                ocean[5 + i, 4:12, cut] = halves[h]
            else:
                frc_s[0, 4 + i : 5 + i, cut] = halves[h][7:8, :]
                frc_s[1, 4 + i : 5 + i, cut] = halves[h][0:1, :]
    frc_copies = [misc(frc_s.at[i], frc_r.at[i], 3 + i, peers[i]) for i in range(2)]
    for side in range(2):
        pl.when(sends[side])(frc_copies[side].start)

    cuts = [slice(0, LANES), slice(LANES, 2 * LANES)]
    masks = [ocean_mask[:, cut] for cut in cuts]
    friction = [
        jnp.sqrt(forcing[0][h] * forcing[0][h] + forcing[1][h] * forcing[1][h] + 0.01) / 1.2
        for h in range(2)
    ]
    for h in range(2):
        state[0, h] = 0.01 * masks[h] * forcing[2][h]
        state[1, h] = 0.01 * masks[h] * forcing[3][h]

    for t in range(STEPS):
        if t > 0:
            sums = advect(t)
        if t == STEPS - 2:
            run_ocean()
        arrived = source(t, sums)
        neighbours = None
        if t == STEPS - 2:
            neighbours = []
            for side in range(2):
                other = 1 - side
                neighbours.append(
                    [
                        [0.01 * spread(frc_r[other, 4 + i : 5 + i, cut]) for cut in cuts]
                        for i in (2, 3)
                    ]
                )
        fluxes = grow(t, neighbours)
        if t < STEPS - 1:
            size = len(fluxes) // 2
            for side in range(2):
                send_flux(t + 1, side, fluxes[size * side : size * side + size])
            move(t + 1, SOON, PARTS)

    for h in range(2):
        energy = fluxes[h] + fluxes[2 + h]
        for side, edge in ((0, 0), (1, 7)):
            extra = state[2, h] * arrived[side][h] + masks[h] * arrived[side][2 + h]
            energy = energy + jnp.where(row8 == edge, extra, 0.0)
        height = 4.0 * jnp.sqrt(energy + 1e-6)
        rough = 1000.0 * ((0.011 + 0.02 * height) * friction[h] / GRAV + 1.5e-5)
        values = [masks[h] * rough, masks[h] * ocean[2, 4:12, cuts[h]], masks[h], zero]
        for i, value in enumerate(values):
            coarse = value.astype(BF16).astype(F32)
            gather[pl.ds(8 * h + i, 8, stride=16), :] = coarse
            gather[pl.ds(8 * h + i + 4, 8, stride=16), :] = value - coarse
    table = gather[...].astype(BF16)

    def to_coarse(at, size, src, tgt):
        part = jnp.dot(table, hot_tgt[:, at], preferred_element_type=F32)
        high = tgt >> 7
        value = jnp.zeros((8, size), F32)
        for h in range(16):
            value = value + jnp.where(high == h, part[8 * h : 8 * h + 8], 0.0)
        value = (value + pltpu.roll(value, 4, 0)) * live_v[:, at]
        value = split_rows(value)
        left = jnp.concatenate([jnp.where((src >> 7) == h, value, 0.0) for h in range(4)], axis=0)
        return lax.dot_general(
            left.astype(BF16), hot_src[:, at], (((1,), (1,)), ((), ())), preferred_element_type=F32
        )

    def joined(value):
        return jnp.concatenate(
            [value[8 * h : 8 * h + 4] + value[8 * h + 4 : 8 * h + 8] for h in range(4)], axis=0
        )

    sum_s[...] = joined(to_coarse(pl.ds(OWN, EDGE), EDGE, esrc_v[...], etgt_v[...]))
    sum_copy = misc(sum_s, sum_r, 5, down_id)
    pl.when(sends[1])(sum_copy.start)

    def back_chunk(c, total):
        at = pl.ds(pl.multiple_of(c * CHUNK, CHUNK), CHUNK)
        return total + to_coarse(at, CHUNK, osrc_v[:, at], otgt_v[:, at])

    own_sums = joined(lax.fori_loop(0, OWN // CHUNK, back_chunk, jnp.zeros((32, LANES), F32)))

    lax.fori_loop(0, PARTS, lambda part, carry: (enter(STEPS - 1, part), carry)[1], 0)

    pl.when(receives[1])(sum_copy.wait_recv)
    totals = own_sums + sum_r[...]
    for h in range(4):
        cut = slice(h * LANES, (h + 1) * LANES)
        share = totals[4 * h + 2 : 4 * h + 3] + 1.0
        drag_out[:, cut] = (totals[4 * h : 4 * h + 1] + 1000.0 * drag_v[:, cut]) / share
        heat_out[:, cut] = (totals[4 * h + 1 : 4 * h + 2] + heat_v[:, cut]) / share

    for side in range(2):
        @pl.when(sends[side])
        def _(side=side):
            for copy in ((atm_copy, sum_copy)[side], sea_copies[side], frc_copies[side]):
                copy.wait_send()
            for t in range(STEPS):
                flux(t, side).wait_send()
                for part in range(PARTS):
                    moving(t, part, side).wait_send()


def write_kernel(el, eh, cur, sst, drag, heat, e_out, cur_out, sst_out, drag_out, heat_out, sems):
    parts = 9
    size = el.shape[0] // parts
    copies = []
    for c in range(parts):
        rows = pl.ds(c * size, size)
        for h, ref in enumerate((el, eh)):
            copies.append((ref.at[rows], e_out.at[rows, pl.ds(h * LANES, LANES)]))
    copies += [(cur, cur_out), (sst, sst_out), (drag, drag_out), (heat, heat_out)]
    copies = [pltpu.make_async_copy(s, d, sems.at[i]) for i, (s, d) in enumerate(copies)]
    for copy in copies:
        copy.start()
    for copy in copies:
        copy.wait()


def per_device(
    axis_sizes, breeze, drag, heat, flow, skin, subs, swell, marine, own_src, own_tgt, own_w,
    edge_src, edge_tgt, edge_w, tally,
):
    ndir, nfreq, rows, columns = swell.shape
    cells = drag.shape[0]
    lines = ndir * nfreq * rows
    rows_view = swell.reshape(ndir, nfreq, rows, 2, LANES).transpose(0, 1, 3, 2, 4)
    rows_view = rows_view.reshape(ndir, nfreq, 2, rows, 1, LANES)
    swell = swell.reshape(lines, columns)
    hbm_spec = pl.BlockSpec(memory_space=pltpu.HBM)
    vmem_spec = pl.BlockSpec(memory_space=pltpu.VMEM)
    small_out = [((2, rows, columns), F32), ((rows, columns), F32), ((1, cells), F32), ((1, cells), F32)]
    vmem = pltpu.VMEM
    dma = pltpu.SemaphoreType.DMA
    results = pl.pallas_call(
        functools.partial(main_kernel, axis_sizes),
        out_shape=[vmem((lines, LANES), F32)] * 2 + [vmem(s, d) for s, d in small_out],
        in_specs=[hbm_spec] * 18,
        out_specs=[vmem_spec] * 6,
        scratch_shapes=[
            vmem(breeze.shape, F32), vmem((1, cells), F32), vmem((1, cells), F32), vmem(flow.shape, F32),
            vmem(skin.shape, F32), vmem(subs.shape, F32), vmem(marine.shape, jnp.int32),
            vmem((1, OWN), jnp.int32), vmem((1, OWN), jnp.int32), vmem((1, OWN), F32),
            vmem((1, EDGE), jnp.int32), vmem((1, EDGE), jnp.int32), vmem((1, EDGE), F32),
            vmem((4, NFREQ, LANES), F32),
            vmem((2, HALF, NFREQ, 2, 1, LANES), F32),
            vmem((STEPS - 1, 2, HALF, 2, NFREQ, LANES), F32),
            vmem((STEPS - 1, 2, HALF, 2, NFREQ, LANES), F32),
            vmem((STEPS, 2, 4, LANES), F32), vmem((STEPS, 2, 4, LANES), F32),
            vmem((16, LANES), F32), vmem((16, LANES), F32),
            vmem((2, 20, columns), F32), vmem((2, 20, columns), F32),
            vmem((2, 8, columns), F32), vmem((2, 8, columns), F32),
            vmem((16, LANES), F32), vmem((16, LANES), F32),
            pltpu.SMEM((4 * NDIR,), F32), pltpu.SMEM((1, 2), jnp.int32),
            vmem((LANES, LIST), BF16), vmem((LANES, LIST), BF16), vmem((1, LIST), F32),
            vmem((LANES, LANES), F32), vmem((7, 16, columns), F32), vmem((4, 2, 8, LANES), F32),
            vmem((LANES, LANES), F32),
            dma((16,)), dma((HALF, 2, 2)),
            dma((STEPS, PARTS, 2)), dma((STEPS, PARTS, 2)),
            dma((STEPS, 2)), dma((STEPS, 2)), dma((6,)), dma((6,)),
        ],
        compiler_params=pltpu.CompilerParams(
            collective_id=0, has_side_effects=True, vmem_limit_bytes=36 * 2**20
        ),
        name="coupled_step",
    )(*(pltpu.with_memory_space_constraint(x, pltpu.HBM) for x in (
        jnp.asarray(direction_table()), tally, swell, rows_view, breeze, drag.reshape(1, cells), heat.reshape(1, cells),
        flow, skin, subs, marine, own_src, own_tgt, own_w, edge_src, edge_tgt, edge_w,
        jnp.asarray(frequency_table()),
    )))
    outs = pl.pallas_call(
        write_kernel,
        out_shape=[jax.ShapeDtypeStruct((lines, columns), F32)]
        + [jax.ShapeDtypeStruct(s, d) for s, d in small_out],
        in_specs=[vmem_spec] * 6,
        out_specs=[hbm_spec] * 5,
        scratch_shapes=[dma((22,))],
        compiler_params=pltpu.CompilerParams(vmem_limit_bytes=4 * 2**20),
        name="write_out",
    )(*(pltpu.with_memory_space_constraint(x, pltpu.VMEM) for x in results))
    spectrum, currents, sst, drag_out, heat_out = outs
    return (
        currents,
        sst,
        spectrum.reshape(ndir, nfreq, rows, columns),
        drag_out.reshape(cells),
        heat_out.reshape(cells),
    )


def solution(mesh):
    both = ("mp", "tile")
    flat, grid, pair = P(both), P(both, None), P(None, both, None)
    in_specs = (P(None, both), flat, flat, pair, grid, grid, P(None, None, both, None)) + (grid,) * 8
    out_specs = (pair, grid, P(None, None, both, None), flat, flat)
    sizes = (mesh.shape["mp"], mesh.shape["tile"])
    return jax.shard_map(
        functools.partial(per_device, sizes), mesh=mesh, in_specs=in_specs, out_specs=out_specs, check_vma=False
    )
```

```python
import functools
import math

import jax
import jax.numpy as jnp
import numpy as np
from jax import lax
from jax.experimental import pallas as pl
from jax.experimental.pallas import tpu as pltpu
from jax.sharding import PartitionSpec as P

MESH = pl.DeviceIdType.MESH
GRAV = 9.81
NDIR = 36
NFREQ = 32
HALF = NDIR // 2
STEPS = 4
LANES = 128
OWN = 4608
EDGE = 384
LIST = OWN + EDGE
CHUNK = 512
AHEAD = 10
PART = 3
PARTS = HALF // PART
EARLY = 2
SOON = 3

F32 = jnp.float32
BF16 = jnp.bfloat16

FREQ = 0.04 * 1.1 ** np.arange(NFREQ)
MU = 0.028 / FREQ
INV_SPEED = 2.0 * math.pi * FREQ / GRAV
WIDTH = 0.1 * FREQ * (2.0 * math.pi / NDIR)
ANGLE = (np.arange(NDIR) + 0.5) * (2.0 * math.pi / NDIR)
COS = np.cos(ANGLE)
SIN = np.sin(ANGLE)


def direction_table():
    return np.stack([COS, SIN, np.abs(COS), np.abs(SIN)], axis=1).reshape(-1).astype(np.float32)


def frequency_table():
    rows = np.stack([MU, INV_SPEED, MU * WIDTH, MU / WIDTH])
    return np.broadcast_to(rows[:, :, None], rows.shape + (LANES,)).astype(np.float32)


def iota(shape, dim):
    return lax.broadcasted_iota(jnp.int32, shape, dim)


def spread(row):
    return jnp.broadcast_to(row, (8, row.shape[-1]))


def split_rows(value):
    coarse = value.astype(BF16).astype(F32)
    return jnp.where(iota(value.shape, 0) < 4, coarse, value - coarse)


def main_kernel(
    axis_sizes,
    dirs_in, tally_in, e_in, e_rows, breeze, drag, heat, flow, skin, subs, marine,
    own_src, own_tgt, own_w, edge_src, edge_tgt, edge_w, freq_in,
    el, eh, cur_out, sst_out, drag_out, heat_out,
    breeze_v, drag_v, heat_v, flow_v, skin_v, subs_v, marine_v,
    osrc_v, otgt_v, ow_v, esrc_v, etgt_v, ew_v, freq,
    first_r, bulk_s, bulk_r, flux_s, flux_r, atm_s, atm_r, sea_s, sea_r, frc_s, frc_r, sum_s, sum_r,
    dirs, tally, hot_src, hot_tgt, live_v, field, ocean, state, gather,
    in_sem, e_sem, bulk_ss, bulk_rs, flux_ss, flux_rs, misc_ss, misc_rs,
):
    mp, tile = lax.axis_index("mp"), lax.axis_index("tile")
    n_mp, n_tile = axis_sizes
    count = n_mp * n_tile
    me = mp * n_tile + tile
    up = lax.rem(me + 1, count)
    down = lax.rem(me + count - 1, count)
    up_id = (lax.div(up, n_tile), lax.rem(up, n_tile))
    down_id = (lax.div(down, n_tile), lax.rem(down, n_tile))
    peers = (up_id, down_id)
    sends = (me < count - 1, me > 0)
    receives = (me > 0, me < count - 1)
    states = (el, eh)

    barrier = pltpu.get_barrier_semaphore()
    for side in range(2):
        @pl.when(sends[side])
        def _(side=side):
            pl.semaphore_signal(barrier, inc=1, device_id=peers[side], device_id_type=MESH)

    small = [
        (breeze, breeze_v), (drag, drag_v), (heat, heat_v), (flow, flow_v), (skin, skin_v),
        (subs, subs_v), (marine, marine_v), (own_src, osrc_v), (own_tgt, otgt_v),
        (own_w, ow_v), (edge_src, esrc_v), (edge_tgt, etgt_v), (edge_w, ew_v),
        (tally_in, tally),
    ]
    small = [(dirs_in, dirs), (freq_in, freq)] + small
    loads = [pltpu.make_async_copy(s, v, in_sem.at[i]) for i, (s, v) in enumerate(small)]
    for load in loads[:9]:
        load.start()

    def e_load(kk, side, half):
        rows = pl.ds(pl.multiple_of((side * HALF + kk) * 256, 256), 256)
        return pltpu.make_async_copy(
            e_in.at[rows, pl.ds(half * LANES, LANES)], states[half].at[rows], e_sem.at[kk, side, half]
        )

    def e_start(kk):
        for side in range(2):
            for half in range(2):
                e_load(kk, side, half).start()

    for kk in range(AHEAD):
        e_start(kk)
    for load in loads[9:]:
        load.start()

    def misc(src, dst, index, peer):
        return pltpu.make_async_remote_copy(
            src, dst, misc_ss.at[index], misc_rs.at[index], device_id=peer, device_id_type=MESH
        )

    for side in range(2):
        @pl.when(jnp.logical_not(receives[side]))
        def _(side=side):
            sea_r[side] = jnp.zeros(sea_r.shape[1:], F32)
            frc_r[side] = jnp.zeros(frc_r.shape[1:], F32)
            for t in range(STEPS):
                flux_r[t, side] = jnp.zeros(flux_r.shape[2:], F32)
            lone = atm_r if side == 0 else sum_r
            lone[...] = jnp.zeros(lone.shape, F32)

    inner = (me > 0) & (me < count - 1)
    pl.semaphore_wait(barrier, jnp.where(inner, 2, 1).astype(jnp.int32))

    def moving(t, part, side):
        at = pl.ds(part * PART, PART)
        if t == 0:
            src = e_rows.at[pl.ds(side * HALF + part * PART, PART), :, :, 7 if side == 0 else 0]
            dst = first_r.at[side, at]
        else:
            src, dst = bulk_s.at[t - 1, side, at], bulk_r.at[t - 1, side, at]
        return pltpu.make_async_remote_copy(
            src, dst, bulk_ss.at[t, part, side], bulk_rs.at[t, part, side],
            device_id=peers[side], device_id_type=MESH,
        )

    def move(t, start, stop):
        for part in range(start, stop):
            for side in range(2):
                pl.when(sends[side])(moving(t, part, side).start)

    move(0, 0, 1)

    def flux(t, side):
        return pltpu.make_async_remote_copy(
            flux_s.at[t, side], flux_r.at[t, side], flux_ss.at[t, side],
            flux_rs.at[t, side], device_id=peers[side], device_id_type=MESH,
        )

    def pack(t, side, kk, totals, neighbour):
        k = side * HALF + kk
        sine = dirs[4 * k + 3]
        coef = 2 if t == 0 else 0
        if neighbour is not None:
            along = [dirs[4 * k] * neighbour[0][h] + dirs[4 * k + 1] * neighbour[1][h] for h in range(2)]
        out = list(totals)
        for g in range(NFREQ // 8):
            weight = freq[coef, 8 * g : 8 * g + 8, :] * sine
            for h in range(2):
                start = k * 256 + 64 * g + (7 if side == 0 else 0)
                rows = states[h][pl.ds(start, 8, stride=8), :]
                if t > 0:
                    bulk_s[t - 1, side, kk, h, 8 * g : 8 * g + 8, :] = rows
                moved = rows * weight
                out[h] = out[h] + moved
                if neighbour is not None:
                    growth = jnp.maximum(along[h] * freq[1, 8 * g : 8 * g + 8, :] - 0.01, 0.0)
                    out[2 + h] = out[2 + h] + moved * growth
        return tuple(out)

    zero = jnp.zeros((8, LANES), F32)

    def send_flux(t, side, totals):
        rows = [jnp.sum(total, axis=0, keepdims=True) for total in totals]
        rows += [jnp.zeros((1, LANES), F32)] * (4 - len(rows))
        flux_s[t, side] = jnp.concatenate(rows, axis=0)
        pl.when(sends[side])(flux(t, side).start)

    def first(kk, carry):
        pl.when(kk + AHEAD < HALF)(lambda: e_start(kk + AHEAD))
        out = []
        for side in range(2):
            for half in range(2):
                e_load(kk, side, half).wait()
            out += list(pack(0, side, kk, carry[2 * side : 2 * side + 2], None))
        return tuple(out)

    for load in loads[2:4]:
        load.wait()
    wind = breeze_v[...]
    east, north = wind[0:1, :], wind[1:2, :]
    factor = 0.4 / jnp.log(10.0 / drag_v[...])
    factor = factor * factor
    speed = jnp.sqrt(east * east + north * north + 1.0)
    for h in range(4):
        cut = slice(h * LANES, (h + 1) * LANES)
        push = 1.2 * factor[:, cut] * speed[:, cut]
        atm_s[4 * h : 4 * h + 1, :] = push * east[:, cut]
        atm_s[4 * h + 1 : 4 * h + 2, :] = push * north[:, cut]
        atm_s[4 * h + 2 : 4 * h + 3, :] = east[:, cut]
        atm_s[4 * h + 3 : 4 * h + 4, :] = north[:, cut]

    atm_copy = misc(atm_s, atm_r, 0, up_id)
    pl.when(sends[0])(atm_copy.start)
    move(0, 1, EARLY)

    for load in loads[:2]:
        load.wait()
    fluxes = lax.fori_loop(0, HALF, first, (zero,) * 4)
    for side in range(2):
        send_flux(0, side, fluxes[2 * side : 2 * side + 2])

    move(0, EARLY, PARTS)

    for load in loads[4:9]:
        load.wait()
    ocean_mask = marine_v[...].astype(F32)
    own_fields = [flow_v[0], flow_v[1], skin_v[...], ocean_mask, subs_v[...]]
    for i, value in enumerate(own_fields):
        sea_s[0, 4 * i : 4 * i + 4, :] = value[4:8, :]
        sea_s[1, 4 * i : 4 * i + 4, :] = value[0:4, :]
        ocean[i, 4:12, :] = value

    sea_copies = [misc(sea_s.at[i], sea_r.at[i], 1 + i, peers[i]) for i in range(2)]
    for side in range(2):
        pl.when(sends[side])(sea_copies[side].start)

    for load in loads[9:]:
        load.wait()

    def to_fine(offset, size, src, tgt, weight, limit, table):
        at = pl.ds(offset, size)
        slot = iota((1, size), 1)
        live = jnp.where(slot < limit, weight, 0.0)
        live_v[:, at] = live
        low = iota((LANES, size), 0)
        hot_s = jnp.where(low == (src & 127), 1.0, 0.0).astype(BF16)
        hot_t = jnp.where(low == (tgt & 127), 1.0, 0.0).astype(BF16)
        hot_src[:, at] = hot_s
        hot_tgt[:, at] = hot_t
        part = jnp.dot(table, hot_s, preferred_element_type=F32)
        part = part[0:16] + part[16:32]
        part = jnp.where((iota((16, size), 0) >> 2) == (src >> 7), part, 0.0)
        part = part[0:8] + part[8:16]
        part = (part + pltpu.roll(part, 4, 0)) * live
        part = split_rows(part)
        high = tgt >> 7
        left = jnp.concatenate([jnp.where(high == h, part, 0.0) for h in range(16)], axis=0)
        return lax.dot_general(
            left.astype(BF16), hot_t, (((1,), (1,)), ((), ())), preferred_element_type=F32
        )

    def two_parts(value):
        coarse = value.astype(BF16).astype(F32)
        return jnp.concatenate([coarse, value - coarse], axis=0).astype(BF16)

    own_table = two_parts(atm_s[...])

    def own_chunk(c, total):
        offset = pl.multiple_of(c * CHUNK, CHUNK)
        at = pl.ds(offset, CHUNK)
        return total + to_fine(
            offset, CHUNK, osrc_v[:, at], otgt_v[:, at], ow_v[:, at], tally[0, 1] - offset, own_table
        )

    row8 = iota((8, LANES), 0)
    lane8 = iota((8, LANES), 1)

    def enter(t, part):
        last = t == STEPS - 1
        coef = 2 if t == 0 else (3 if last else 0)
        def one(kk, carry, side):
            edge = 0 if side == 0 else 7
            k = side * HALF + kk
            sine = dirs[4 * k + 3]
            rows = [[spread(state[i, h, edge : edge + 1, :]) for h in range(2)] for i in range(4)]
            along = [dirs[4 * k] * rows[0][h] + dirs[4 * k + 1] * rows[1][h] for h in range(2)]
            for g in range(NFREQ // 8):
                cut = slice(8 * g, 8 * g + 8)
                weight = freq[coef, cut, :] * sine
                for h in range(2):
                    grown = jnp.maximum(along[h] * freq[1, cut, :] + rows[3][h], rows[2][h])
                    at = pl.ds(k * 256 + 64 * g + edge, 8, stride=8)
                    if t == 0:
                        came = first_r[side, kk, cut, h, 0, :]
                    else:
                        came = bulk_r[t - 1, side, kk, h, cut, :]
                    states[h][at, :] = states[h][at, :] + came * weight * grown
            return carry

        for side in range(2):
            @pl.when(receives[side])
            def _(side=side):
                moving(t, part, side).wait_recv()
                lax.fori_loop(part * PART, part * PART + PART, functools.partial(one, side=side), 0)

    def advect(t):
        sums = (zero,) * 4
        for pair in range(2):
            def one(kk, sums, side, pair=pair):
                west = side == pair
                south = side == 0
                k = side * HALF + kk
                cosine, sine = dirs[4 * k + 2], dirs[4 * k + 3]
                both = cosine + sine
                if west:
                    cos_l = jnp.where(lane8 > 0, cosine, 0.0)
                    cos_h = jnp.full((8, LANES), cosine, F32)
                else:
                    cos_l = jnp.full((8, LANES), cosine, F32)
                    cos_h = jnp.where(lane8 < LANES - 1, cosine, 0.0)
                sin_v = jnp.where(row8 > 0 if south else row8 < 7, sine, 0.0)
                sums = list(sums)
                for m in range(NFREQ):
                    rows = pl.ds(pl.multiple_of(k * 256 + m * 8, 8), 8)
                    e_l, e_h = el[rows, :], eh[rows, :]
                    turn = 1 if west else LANES - 1
                    r_l, r_h = pltpu.roll(e_l, turn, 1), pltpu.roll(e_h, turn, 1)
                    if west:
                        x_l, x_h = r_l, jnp.where(lane8 == 0, r_l, r_h)
                    else:
                        x_l, x_h = jnp.where(lane8 == LANES - 1, r_h, r_l), r_h
                    shift = 1 if south else 7
                    y_l, y_h = pltpu.roll(e_l, shift, 0), pltpu.roll(e_h, shift, 0)
                    scale = float(WIDTH[m]) if t == 0 else 1.0
                    keep = scale - (scale * float(MU[m])) * both
                    gain = scale * float(MU[m])
                    a_l = keep * e_l + gain * (cos_l * x_l + sin_v * y_l)
                    a_h = keep * e_h + gain * (cos_h * x_h + sin_v * y_h)
                    el[rows, :] = a_l
                    eh[rows, :] = a_h
                    p = 2 * (m % 2)
                    sums[p] = sums[p] + a_l
                    sums[p + 1] = sums[p + 1] + a_h
                return tuple(sums)

            def part(p, sums, pair=pair, one=one):
                p = p + pair * (PARTS // 2)
                if t > 0:
                    enter(t - 1, p)
                for side in range(2):
                    sums = lax.fori_loop(p * PART, p * PART + PART, functools.partial(one, side=side), sums)
                return sums

            sums = lax.fori_loop(0, PARTS // 2, part, sums)
        return [sums[0] + sums[2], sums[1] + sums[3]]

    def source(t, sums):
        for side in range(2):
            pl.when(receives[side])(flux(t, side).wait_recv)
        arrived = []
        for side in range(2):
            arrived.append(
                [spread(flux_r[t, side, i : i + 1, :]) for i in range(4)]
            )
        for h in range(2):
            energy = sums[h] + jnp.where(row8 == 0, arrived[0][h], 0.0)
            energy = energy + jnp.where(row8 == 7, arrived[1][h], 0.0)
            kept = masks[h] * (1.0 - 0.3 * energy / (energy + 1.0))
            state[2, h] = kept
            state[3, h] = kept - 0.01 * masks[h]
        return arrived

    def grow(t, neighbours):
        last = t == STEPS - 1

        def one(kk, carry):
            out = []
            for side in range(2):
                k = side * HALF + kk
                cosine, sine = dirs[4 * k], dirs[4 * k + 1]
                along = [cosine * state[0, h] + sine * state[1, h] for h in range(2)]
                kept = [state[2, h] for h in range(2)]
                base = [state[3, h] for h in range(2)]
                size = len(carry) // 2
                totals = list(carry[size * side : size * side + size])
                for m in range(NFREQ):
                    rows = pl.ds(pl.multiple_of(k * 256 + m * 8, 8), 8)
                    for h in range(2):
                        grown = jnp.maximum(along[h] * float(INV_SPEED[m]) + base[h], kept[h])
                        value = states[h][rows, :] * grown
                        if last:
                            totals[h] = totals[h] + value
                            value = value * float(1.0 / WIDTH[m])
                        states[h][rows, :] = value
                if not last:
                    totals = pack(t + 1, side, kk, totals, neighbours[side] if neighbours else None)
                out += list(totals)
            return tuple(out)

        totals = (zero,) * (8 if neighbours else 4)
        if last:
            return lax.fori_loop(0, HALF, one, totals)
        totals = lax.fori_loop(0, SOON * PART, one, totals)
        move(t + 1, 0, SOON)
        return lax.fori_loop(SOON * PART, HALF, one, totals)

    def run_ocean():
        for side in range(2):
            pl.when(receives[side])(sea_copies[side].wait_recv)
            pl.when(receives[side])(frc_copies[side].wait_recv)
        for side, first in ((0, 0), (1, 12)):
            for i in range(5):
                ocean[i, first : first + 4, :] = sea_r[side, 4 * i : 4 * i + 4, :]
            for i in range(2):
                inner_row = first + 1 if side == 0 else first
                ocean[5 + i, inner_row : inner_row + 3, :] = frc_r[side, 3 * i : 3 * i + 3, :]
                outer_row = first if side == 0 else first + 3
                ocean[5 + i, outer_row : outer_row + 1, :] = jnp.zeros((1, 2 * LANES), F32)
        u, v, q = ocean[0], ocean[1], ocean[2]
        wet, deep, push_u, push_v = ocean[3], ocean[4], ocean[5], ocean[6]
        rub = 0.05 * (jnp.sqrt(push_u * push_u + push_v * push_v + 0.01) / 1.2)
        lane = iota((16, 2 * LANES), 1)

        def lap(w):
            west = jnp.where(lane == 0, 0.0, pltpu.roll(w, 1, 1))
            east = jnp.where(lane == 2 * LANES - 1, 0.0, pltpu.roll(w, 2 * LANES - 1, 1))
            return pltpu.roll(w, 1, 0) + pltpu.roll(w, 15, 0) + west + east - 4.0 * w

        for _ in range(STEPS):
            u, v, q = (
                wet * (u + 0.1 * push_u + 0.2 * v - 0.05 * u + 0.2 * lap(u)),
                wet * (v + 0.1 * push_v - 0.2 * u - 0.05 * v + 0.2 * lap(v)),
                wet * (q + 0.2 * lap(q) - rub * (q - deep)),
            )
        ocean[0], ocean[1], ocean[2] = u, v, q
        cur_out[0] = ocean[0, 4:12, :]
        cur_out[1] = ocean[1, 4:12, :]
        sst_out[...] = ocean[2, 4:12, :]

    total = lax.fori_loop(0, OWN // CHUNK, own_chunk, jnp.zeros((LANES, LANES), F32))
    sums = advect(0)
    pl.when(receives[0])(atm_copy.wait_recv)
    edge_limit = jnp.where(me > 0, tally[0, 0], 0)
    total = total + to_fine(
        OWN, EDGE, esrc_v[...], etgt_v[...], ew_v[...], edge_limit, two_parts(atm_r[...])
    )
    field[...] = total
    forcing = []
    for i in range(4):
        halves = []
        for h in range(2):
            coarse = field[pl.ds(8 * h + i, 8, stride=16), :]
            halves.append(coarse + field[pl.ds(8 * h + i + 4, 8, stride=16), :])
        forcing.append(halves)
        for h in range(2):
            cut = slice(h * LANES, (h + 1) * LANES)
            if i < 2:
                frc_s[0, 3 * i : 3 * i + 3, cut] = halves[h][5:8, :]
                frc_s[1, 3 * i : 3 * i + 3, cut] = halves[h][0:3, :]
                ocean[5 + i, 4:12, cut] = halves[h]
            else:
                frc_s[0, 4 + i : 5 + i, cut] = halves[h][7:8, :]
                frc_s[1, 4 + i : 5 + i, cut] = halves[h][0:1, :]
    frc_copies = [misc(frc_s.at[i], frc_r.at[i], 3 + i, peers[i]) for i in range(2)]
    for side in range(2):
        pl.when(sends[side])(frc_copies[side].start)

    cuts = [slice(0, LANES), slice(LANES, 2 * LANES)]
    masks = [ocean_mask[:, cut] for cut in cuts]
    friction = [
        jnp.sqrt(forcing[0][h] * forcing[0][h] + forcing[1][h] * forcing[1][h] + 0.01) / 1.2
        for h in range(2)
    ]
    for h in range(2):
        state[0, h] = 0.01 * masks[h] * forcing[2][h]
        state[1, h] = 0.01 * masks[h] * forcing[3][h]

    for t in range(STEPS):
        if t > 0:
            sums = advect(t)
        if t == STEPS - 2:
            run_ocean()
        arrived = source(t, sums)
        neighbours = None
        if t == STEPS - 2:
            neighbours = []
            for side in range(2):
                other = 1 - side
                neighbours.append(
                    [
                        [0.01 * spread(frc_r[other, 4 + i : 5 + i, cut]) for cut in cuts]
                        for i in (2, 3)
                    ]
                )
        fluxes = grow(t, neighbours)
        if t < STEPS - 1:
            size = len(fluxes) // 2
            for side in range(2):
                send_flux(t + 1, side, fluxes[size * side : size * side + size])
            move(t + 1, SOON, PARTS)

    for h in range(2):
        energy = fluxes[h] + fluxes[2 + h]
        for side, edge in ((0, 0), (1, 7)):
            extra = state[2, h] * arrived[side][h] + masks[h] * arrived[side][2 + h]
            energy = energy + jnp.where(row8 == edge, extra, 0.0)
        height = 4.0 * jnp.sqrt(energy + 1e-6)
        rough = 1000.0 * ((0.011 + 0.02 * height) * friction[h] / GRAV + 1.5e-5)
        values = [masks[h] * rough, masks[h] * ocean[2, 4:12, cuts[h]], masks[h], zero]
        for i, value in enumerate(values):
            coarse = value.astype(BF16).astype(F32)
            gather[pl.ds(8 * h + i, 8, stride=16), :] = coarse
            gather[pl.ds(8 * h + i + 4, 8, stride=16), :] = value - coarse
    table = gather[...].astype(BF16)

    def to_coarse(at, size, src, tgt):
        part = jnp.dot(table, hot_tgt[:, at], preferred_element_type=F32)
        high = tgt >> 7
        value = jnp.zeros((8, size), F32)
        for h in range(16):
            value = value + jnp.where(high == h, part[8 * h : 8 * h + 8], 0.0)
        value = (value + pltpu.roll(value, 4, 0)) * live_v[:, at]
        value = split_rows(value)
        left = jnp.concatenate([jnp.where((src >> 7) == h, value, 0.0) for h in range(4)], axis=0)
        return lax.dot_general(
            left.astype(BF16), hot_src[:, at], (((1,), (1,)), ((), ())), preferred_element_type=F32
        )

    def joined(value):
        return jnp.concatenate(
            [value[8 * h : 8 * h + 4] + value[8 * h + 4 : 8 * h + 8] for h in range(4)], axis=0
        )

    sum_s[...] = joined(to_coarse(pl.ds(OWN, EDGE), EDGE, esrc_v[...], etgt_v[...]))
    sum_copy = misc(sum_s, sum_r, 5, down_id)
    pl.when(sends[1])(sum_copy.start)

    def back_chunk(c, total):
        at = pl.ds(pl.multiple_of(c * CHUNK, CHUNK), CHUNK)
        return total + to_coarse(at, CHUNK, osrc_v[:, at], otgt_v[:, at])

    own_sums = joined(lax.fori_loop(0, OWN // CHUNK, back_chunk, jnp.zeros((32, LANES), F32)))

    lax.fori_loop(0, PARTS, lambda part, carry: (enter(STEPS - 1, part), carry)[1], 0)

    pl.when(receives[1])(sum_copy.wait_recv)
    totals = own_sums + sum_r[...]
    for h in range(4):
        cut = slice(h * LANES, (h + 1) * LANES)
        share = totals[4 * h + 2 : 4 * h + 3] + 1.0
        drag_out[:, cut] = (totals[4 * h : 4 * h + 1] + 1000.0 * drag_v[:, cut]) / share
        heat_out[:, cut] = (totals[4 * h + 1 : 4 * h + 2] + heat_v[:, cut]) / share

    for side in range(2):
        @pl.when(sends[side])
        def _(side=side):
            for copy in ((atm_copy, sum_copy)[side], sea_copies[side], frc_copies[side]):
                copy.wait_send()
            for t in range(STEPS):
                flux(t, side).wait_send()
                for part in range(PARTS):
                    moving(t, part, side).wait_send()


def write_kernel(el, eh, cur, sst, drag, heat, e_out, cur_out, sst_out, drag_out, heat_out, sems):
    parts = 9
    size = el.shape[0] // parts
    copies = []
    for c in range(parts):
        rows = pl.ds(c * size, size)
        for h, ref in enumerate((el, eh)):
            copies.append((ref.at[rows], e_out.at[rows, pl.ds(h * LANES, LANES)]))
    copies += [(cur, cur_out), (sst, sst_out), (drag, drag_out), (heat, heat_out)]
    copies = [pltpu.make_async_copy(s, d, sems.at[i]) for i, (s, d) in enumerate(copies)]
    for copy in copies:
        copy.start()
    for copy in copies:
        copy.wait()


def per_device(
    axis_sizes, breeze, drag, heat, flow, skin, subs, swell, marine, own_src, own_tgt, own_w,
    edge_src, edge_tgt, edge_w, tally,
):
    ndir, nfreq, rows, columns = swell.shape
    cells = drag.shape[0]
    lines = ndir * nfreq * rows
    rows_view = swell.reshape(ndir, nfreq, rows, 2, LANES).transpose(0, 1, 3, 2, 4)
    rows_view = rows_view.reshape(ndir, nfreq, 2, rows, 1, LANES)
    swell = swell.reshape(lines, columns)
    hbm_spec = pl.BlockSpec(memory_space=pltpu.HBM)
    vmem_spec = pl.BlockSpec(memory_space=pltpu.VMEM)
    small_out = [((2, rows, columns), F32), ((rows, columns), F32), ((1, cells), F32), ((1, cells), F32)]
    vmem = pltpu.VMEM
    dma = pltpu.SemaphoreType.DMA
    results = pl.pallas_call(
        functools.partial(main_kernel, axis_sizes),
        out_shape=[vmem((lines, LANES), F32)] * 2 + [vmem(s, d) for s, d in small_out],
        in_specs=[hbm_spec] * 18,
        out_specs=[vmem_spec] * 6,
        scratch_shapes=[
            vmem(breeze.shape, F32), vmem((1, cells), F32), vmem((1, cells), F32), vmem(flow.shape, F32),
            vmem(skin.shape, F32), vmem(subs.shape, F32), vmem(marine.shape, jnp.int32),
            vmem((1, OWN), jnp.int32), vmem((1, OWN), jnp.int32), vmem((1, OWN), F32),
            vmem((1, EDGE), jnp.int32), vmem((1, EDGE), jnp.int32), vmem((1, EDGE), F32),
            vmem((4, NFREQ, LANES), F32),
            vmem((2, HALF, NFREQ, 2, 1, LANES), F32),
            vmem((STEPS - 1, 2, HALF, 2, NFREQ, LANES), F32),
            vmem((STEPS - 1, 2, HALF, 2, NFREQ, LANES), F32),
            vmem((STEPS, 2, 4, LANES), F32), vmem((STEPS, 2, 4, LANES), F32),
            vmem((16, LANES), F32), vmem((16, LANES), F32),
            vmem((2, 20, columns), F32), vmem((2, 20, columns), F32),
            vmem((2, 8, columns), F32), vmem((2, 8, columns), F32),
            vmem((16, LANES), F32), vmem((16, LANES), F32),
            pltpu.SMEM((4 * NDIR,), F32), pltpu.SMEM((1, 2), jnp.int32),
            vmem((LANES, LIST), BF16), vmem((LANES, LIST), BF16), vmem((1, LIST), F32),
            vmem((LANES, LANES), F32), vmem((7, 16, columns), F32), vmem((4, 2, 8, LANES), F32),
            vmem((LANES, LANES), F32),
            dma((16,)), dma((HALF, 2, 2)),
            dma((STEPS, PARTS, 2)), dma((STEPS, PARTS, 2)),
            dma((STEPS, 2)), dma((STEPS, 2)), dma((6,)), dma((6,)),
        ],
        compiler_params=pltpu.CompilerParams(
            collective_id=0, has_side_effects=True, vmem_limit_bytes=36 * 2**20
        ),
        name="coupled_step",
    )(*(pltpu.with_memory_space_constraint(x, pltpu.HBM) for x in (
        jnp.asarray(direction_table()), tally, swell, rows_view, breeze, drag.reshape(1, cells), heat.reshape(1, cells),
        flow, skin, subs, marine, own_src, own_tgt, own_w, edge_src, edge_tgt, edge_w,
        jnp.asarray(frequency_table()),
    )))
    outs = pl.pallas_call(
        write_kernel,
        out_shape=[jax.ShapeDtypeStruct((lines, columns), F32)]
        + [jax.ShapeDtypeStruct(s, d) for s, d in small_out],
        in_specs=[vmem_spec] * 6,
        out_specs=[hbm_spec] * 5,
        scratch_shapes=[dma((22,))],
        compiler_params=pltpu.CompilerParams(vmem_limit_bytes=4 * 2**20),
        name="write_out",
    )(*(pltpu.with_memory_space_constraint(x, pltpu.VMEM) for x in results))
    spectrum, currents, sst, drag_out, heat_out = outs
    return (
        currents,
        sst,
        spectrum.reshape(ndir, nfreq, rows, columns),
        drag_out.reshape(cells),
        heat_out.reshape(cells),
    )


def solution(mesh):
    both = ("mp", "tile")
    flat, grid, pair = P(both), P(both, None), P(None, both, None)
    in_specs = (P(None, both), flat, flat, pair, grid, grid, P(None, None, both, None)) + (grid,) * 8
    out_specs = (pair, grid, P(None, None, both, None), flat, flat)
    sizes = (mesh.shape["mp"], mesh.shape["tile"])
    return jax.shard_map(
        functools.partial(per_device, sizes), mesh=mesh, in_specs=in_specs, out_specs=out_specs, check_vma=False
    )
```
